32 devices in a mesh: seq: 8 (over z, x), head: 4 (over y, core).
Axes of the slice: x: 2, y: 2, z: 4, core: 2. Of those that a mesh axis runs over, the one named last changes fastest.
Arguments:
- query: bfloat16 [2048, 1024], P('seq', 'head'), may hold values from -20 to 20
- key_states: bfloat16 [2048, 1024], P('seq', 'head'), may hold values from -20 to 20
- values: bfloat16 [2048, 1024], P('seq', 'head'), may hold values from -6 to 6
- grad_out: bfloat16 [2048, 1024], P('seq', 'head'), may hold values from -6 to 6
- rand_blocks: int32 [32, 2], replicated, may hold values from 0 to 31, as said below
- global_blocks: int32 [2], replicated, may hold values from 0 to 31, as said below
Outputs:
- out: bfloat16 [2048, 1024], P('seq', 'head')
- dq: bfloat16 [2048, 1024], P('seq', 'head')
- dk: bfloat16 [2048, 1024], P('seq', 'head')
- dv: bfloat16 [2048, 1024], P('seq', 'head')
The draws below stay inside these ranges and needn't reach their ends.
Inputs may be any that keep to these rules, and one draw needn't show every extreme that they name: `rand_blocks`: take the query blocks of one index of seq (aligned runs of 4 rows). Among their 8 entries at most 2 lie in the blocks of any one index o (blocks o*4 to o*4 + 3), and for every run some index receives exactly 2 of them. `global_blocks`: 2 different block numbers; the last of them is the sequence's last block.
All inputs are finite; a program needn't handle non-finite values.
Results may differ from the reference program's by a relative error of at most 0.04.
Values may be sent and summed in bfloat16 or wider, within the bound.
A program may use at most 128 MiB of HBM per device.

```python
import math
import jax
import jax.numpy as jnp
from jax import lax

HEAD_SIZE = 128
HEADS = 8
BLOCK_TOKENS = 64
GLOB = 2
RAND = 2
QB = 4
NBLK = 32
SEQ = 2048
CAP = 2


def draw_query(key, part):
    drawn = jnp.clip(jax.random.normal(jax.random.fold_in(key, 21), (SEQ, HEADS * HEAD_SIZE), jnp.float32), -6.0, 6.0)
    return drawn.astype(jnp.bfloat16)


def draw_key_states(key, part):
    drawn = jnp.clip(jax.random.normal(jax.random.fold_in(key, 31), (SEQ, HEADS * HEAD_SIZE), jnp.float32), -6.0, 6.0)
    return drawn.astype(jnp.bfloat16)


def draw_rand_blocks(key, part):
    shards = NBLK // QB
    needed = QB * RAND
    seats = shards * CAP
    hot_owner = jax.random.randint(jax.random.fold_in(key, 41), (shards,), 0, shards)
    seat_owner = jnp.arange(seats) // CAP
    seat_scores = jax.random.randint(jax.random.fold_in(key, 42), (shards, seats), 0, 1 << 12) * seats + jnp.arange(seats)[None, :]
    seat_scores = seat_scores + (seat_owner[None, :] == hot_owner[:, None]).astype(jnp.int32) * ((1 << 12) * seats)
    order = jnp.argsort(seat_scores, axis=1)
    picked = seat_owner[order[:, :needed - CAP]]
    owners = jnp.concatenate([jnp.broadcast_to(hot_owner[:, None], (shards, CAP)), picked], axis=1)
    mix_scores = jax.random.randint(jax.random.fold_in(key, 43), (shards, needed), 0, 1 << 12) * needed + jnp.arange(needed)[None, :]
    owners = jnp.take_along_axis(owners, jnp.argsort(mix_scores, axis=1), axis=1)
    local = jax.random.randint(jax.random.fold_in(key, 44), (shards, needed), 0, QB)
    return (owners * QB + local).astype(jnp.int32).reshape(NBLK, RAND)


def draw_global_blocks(key, part):
    others = jax.random.permutation(jax.random.fold_in(key, 51), NBLK - 1)[:GLOB - 1].astype(jnp.int32)
    return jnp.concatenate([others, jnp.full((1,), NBLK - 1, jnp.int32)]).astype(jnp.int32)


def shard_levels(rng, dims, cuts, least, high):
    def one(dim, shards_of):
        steps = jax.random.uniform(jax.random.fold_in(jax.random.fold_in(rng, 6), dim), (shards_of,), jnp.float32, least / len(cuts), high / len(cuts))
        return jnp.repeat(jnp.exp(steps), dims[dim] // shards_of).reshape((-1,) + (1,) * (len(dims) - dim - 1))

    level = one(*cuts[0])
    for cut in cuts[1:]:
        level = level * one(*cut)
    return level


def scatter_about(stream_key, shape, scale, bound, cuts=(), held_as=jnp.bfloat16):
    result = scale * jax.random.normal(stream_key, shape, jnp.float32)
    if cuts:
        result = result * shard_levels(stream_key, shape, cuts, -0.22, 0.18)
    return jnp.clip(result, -bound, bound).astype(held_as)


def setup_inputs(seed: int = 0) -> dict:
    splits = jax.random.split(jax.random.key(seed), 7)
    return {
        "query": draw_query(jax.random.fold_in(splits[6], 71), 0),
        "key_states": draw_key_states(jax.random.fold_in(splits[6], 71), 0),
        "values": scatter_about(splits[2], (SEQ, HEADS * HEAD_SIZE), 1.0, 6.0, ((0, 8), (1, 4))),
        "grad_out": scatter_about(splits[3], (SEQ, HEADS * HEAD_SIZE), 1.0, 6.0, ((0, 8), (1, 4))),
        "rand_blocks": draw_rand_blocks(jax.random.fold_in(splits[6], 71), 0),
        "global_blocks": draw_global_blocks(jax.random.fold_in(splits[6], 71), 0),
    }


def key_lists(rand_blocks, global_blocks):
    block_count = rand_blocks.shape[0]
    order = jnp.arange(block_count, dtype=jnp.int32)
    window = jnp.stack([(order - 1) % block_count, order, (order + 1) % block_count], axis=1)
    globals_wide = jnp.broadcast_to(global_blocks.astype(jnp.int32)[None, :], (block_count, global_blocks.shape[0]))
    return jnp.concatenate([window, globals_wide, rand_blocks.astype(jnp.int32)], axis=1)

def reference(query, key_states, values, grad_out, rand_blocks, global_blocks):
    lists = key_lists(rand_blocks, global_blocks)
    block_count = lists.shape[0]
    key_count = lists.shape[1]
    nfixed = 3 + GLOB
    score_scale = 1.0 / math.sqrt(HEAD_SIZE)

    def per_head(arrays):
        head_query, head_keys, head_values, head_grad = arrays
        query_matrix = head_query.reshape(block_count, BLOCK_TOKENS, HEAD_SIZE).astype(jnp.float32)
        key_blocks = head_keys.reshape(block_count, BLOCK_TOKENS, HEAD_SIZE)
        value_blocks = head_values.reshape(block_count, BLOCK_TOKENS, HEAD_SIZE)
        key_matrix = key_blocks[lists].reshape(block_count, key_count * BLOCK_TOKENS, HEAD_SIZE).astype(jnp.float32)
        value_matrix = value_blocks[lists].reshape(block_count, key_count * BLOCK_TOKENS, HEAD_SIZE).astype(jnp.float32)
        logit_scores = jnp.einsum('tjo,two->tjw', query_matrix, key_matrix) * score_scale
        top = lax.optimization_barrier(jnp.max(logit_scores, axis=-1, keepdims=True))
        lse = top + jnp.log(lax.optimization_barrier(jnp.sum(jnp.exp(logit_scores - top), axis=-1, keepdims=True)))
        probs = jnp.exp(logit_scores - lse)
        softmax_weights = probs.astype(jnp.bfloat16)
        attended_output = jnp.einsum('zyg,zgu->zyu', softmax_weights.astype(jnp.float32), value_matrix).astype(jnp.bfloat16)
        gradient_rows = head_grad.reshape(block_count, BLOCK_TOKENS, HEAD_SIZE).astype(jnp.float32)
        delta = lax.optimization_barrier(jnp.sum(gradient_rows * attended_output.astype(jnp.float32), axis=-1, keepdims=True))
        probability_gradient = jnp.einsum('tjo,two->tjw', gradient_rows, value_matrix)
        dscore = (probs * (probability_gradient - delta) * score_scale).astype(jnp.bfloat16)
        score_gradient_wide = dscore.astype(jnp.float32)
        query_gradient = jnp.einsum('zyg,zgu->zyu', score_gradient_wide, key_matrix).astype(jnp.bfloat16)
        key_term = jnp.einsum('zgu,zgf->zuf', score_gradient_wide, query_matrix).reshape(block_count, key_count, BLOCK_TOKENS, HEAD_SIZE)
        value_term = jnp.einsum('zgu,zgf->zuf', softmax_weights.astype(jnp.float32), gradient_rows).reshape(block_count, key_count, BLOCK_TOKENS, HEAD_SIZE)
        k_random = lax.optimization_barrier(key_term[:, nfixed:].astype(jnp.bfloat16)).astype(jnp.float32)
        v_random = lax.optimization_barrier(value_term[:, nfixed:].astype(jnp.bfloat16)).astype(jnp.float32)
        key_term = jnp.concatenate([key_term[:, :nfixed], k_random], axis=1)
        value_term = jnp.concatenate([value_term[:, :nfixed], v_random], axis=1)
        dkey = jnp.zeros((block_count, BLOCK_TOKENS, HEAD_SIZE), jnp.float32).at[lists].add(key_term)
        dvalue = jnp.zeros((block_count, BLOCK_TOKENS, HEAD_SIZE), jnp.float32).at[lists].add(value_term)
        return (attended_output.reshape(SEQ, HEAD_SIZE), query_gradient.reshape(SEQ, HEAD_SIZE), dkey.astype(jnp.bfloat16).reshape(SEQ, HEAD_SIZE), dvalue.astype(jnp.bfloat16).reshape(SEQ, HEAD_SIZE))

    def split_heads(array):
        return jnp.transpose(array.reshape(SEQ, HEADS, HEAD_SIZE), (1, 0, 2))

    def join_heads(array):
        return jnp.transpose(array, (1, 0, 2)).reshape(SEQ, HEADS * HEAD_SIZE)
    results = lax.map(per_head, (split_heads(query), split_heads(key_states), split_heads(values), split_heads(grad_out)))
    return (join_heads(results[0]), join_heads(results[1]), join_heads(results[2]), join_heads(results[3]))
```

```python
import math

import jax
import jax.numpy as jnp
from jax import lax
from jax.experimental import pallas as pl
from jax.experimental.pallas import tpu as pltpu
from jax.sharding import PartitionSpec as P

HEAD_SIZE = 128
BLOCK_TOKENS = 64


def extended_2(block, sides, width):
    for axis, dim in sides:
        count = lax.axis_size(axis)
        forward = [(i, i + 1) for i in range(count - 1)]
        forward.append((count - 1, 0))
        backward = [(target, source) for source, target in forward]
        low = lax.ppermute(
            lax.slice_in_dim(block, block.shape[dim] - width, None, axis=dim), axis, forward
        )
        high = lax.ppermute(lax.slice_in_dim(block, 0, width, axis=dim), axis, backward)
        block = jnp.concatenate([low, block, high], axis=dim)
    return block


def pick_blocks(blocks, index):
    onehot = (index[..., None] == jnp.arange(blocks.shape[0])).astype(blocks.dtype)
    picked = jnp.einsum(
        "...b,bqc->...qc", onehot, blocks, preferred_element_type=jnp.float32
    )
    return picked.astype(blocks.dtype)


def shards(query, key_states, values, grad_out, rand_blocks, global_blocks):
    tokens, feature_width = query.shape
    head_count = feature_width // HEAD_SIZE
    nshard = lax.axis_size("seq")
    myself = lax.axis_index("seq")
    block_count = tokens // BLOCK_TOKENS
    nrand = rand_blocks.shape[1]
    nglob = global_blocks.shape[0]
    nfixed = 3 + nglob
    needed = block_count * nrand
    slots = max(2, (needed + nshard - 1) // nshard)
    double_width = 2 * feature_width
    score_scale = 1.0 / math.sqrt(HEAD_SIZE)
    paired = jnp.concatenate([key_states, values], axis=1)
    paired_blocks = paired.reshape(block_count, BLOCK_TOKENS, double_width)
    extended = extended_2(paired, (("seq", 0),), BLOCK_TOKENS)
    owners_glob = global_blocks // block_count
    local_glob = global_blocks % block_count
    pieces = []
    for glob_index in range(nglob):
        piece = lax.dynamic_slice_in_dim(
            paired, local_glob[glob_index] * BLOCK_TOKENS, BLOCK_TOKENS, 0
        )
        pieces.append(jnp.where(owners_glob[glob_index] == myself, piece.astype(jnp.float32), 0.0))
    global_rows = lax.psum(jnp.concatenate(pieces, axis=0), "seq").astype(jnp.bfloat16)
    table = rand_blocks.reshape(nshard, needed)
    owner_table = table // block_count
    local_table = table % block_count
    position = jnp.arange(needed)
    earlier_same = (owner_table[:, :, None] == owner_table[:, None, :]) & (
        position[None, None, :] < position[None, :, None]
    )
    rank_table = jnp.sum(earlier_same.astype(jnp.int32), axis=2)
    slot_range = jnp.arange(slots)
    matched = (owner_table[:, :, None] == myself) & (
        rank_table[:, :, None] == slot_range[None, None, :]
    )
    valid = jnp.any(matched, axis=1)
    send_local = jnp.sum(jnp.where(matched, local_table[:, :, None], 0), axis=1)
    outgoing = jnp.where(
        valid[:, :, None, None], pick_blocks(paired_blocks, send_local), jnp.zeros((), jnp.bfloat16)
    )
    incoming = lax.all_to_all(outgoing, "seq", split_axis=0, concat_axis=0, tiled=True)
    my_owner = lax.dynamic_index_in_dim(owner_table, myself, 0, keepdims=False)
    my_rank = lax.dynamic_index_in_dim(rank_table, myself, 0, keepdims=False)
    flat_slot = my_owner * slots + my_rank
    fetched = pick_blocks(
        incoming.reshape(nshard * slots, BLOCK_TOKENS, double_width), flat_slot
    ).reshape(block_count, nrand, BLOCK_TOKENS, double_width)
    ext_blocks = extended.reshape(block_count + 2, BLOCK_TOKENS, double_width)
    window_blocks = jnp.stack([ext_blocks[:-2], ext_blocks[1:-1], ext_blocks[2:]], axis=1)
    glob_wide = jnp.broadcast_to(
        global_rows.reshape(1, nglob, BLOCK_TOKENS, double_width),
        (block_count, nglob, BLOCK_TOKENS, double_width),
    )
    gathered = jnp.concatenate([window_blocks, glob_wide, fetched], axis=1)
    key_count = gathered.shape[1]
    key_matrix = gathered[..., :feature_width].reshape(
        block_count, key_count * BLOCK_TOKENS, head_count, HEAD_SIZE
    )
    value_matrix = gathered[..., feature_width:].reshape(
        block_count, key_count * BLOCK_TOKENS, head_count, HEAD_SIZE
    )
    query_matrix = query.reshape(block_count, BLOCK_TOKENS, head_count, HEAD_SIZE)
    logit_scores = (
        jnp.einsum("bqhd,bkhd->bhqk", query_matrix, key_matrix, preferred_element_type=jnp.float32)
        * score_scale
    )
    top = jnp.max(logit_scores, axis=-1, keepdims=True)
    lse = top + jnp.log(jnp.sum(jnp.exp(logit_scores - top), axis=-1, keepdims=True))
    probs = jnp.exp(logit_scores - lse)
    softmax_weights = probs.astype(jnp.bfloat16)
    attended_output = jnp.einsum(
        "bhqk,bkhd->bqhd", softmax_weights, value_matrix, preferred_element_type=jnp.float32
    ).astype(jnp.bfloat16)
    out = attended_output.reshape(tokens, feature_width)
    gradient_rows = grad_out.reshape(block_count, BLOCK_TOKENS, head_count, HEAD_SIZE)
    delta = jnp.sum(gradient_rows.astype(jnp.float32) * attended_output.astype(jnp.float32), axis=3)
    delta = jnp.transpose(delta, (0, 2, 1))[..., None]
    probability_gradient = jnp.einsum(
        "bqhd,bkhd->bhqk", gradient_rows, value_matrix, preferred_element_type=jnp.float32
    )
    dscore = (probs * (probability_gradient - delta) * score_scale).astype(jnp.bfloat16)
    query_gradient = jnp.einsum(
        "bhqk,bkhd->bqhd", dscore, key_matrix, preferred_element_type=jnp.float32
    ).astype(jnp.bfloat16)
    query_gradient = query_gradient.reshape(tokens, feature_width)
    key_term = jnp.einsum(
        "bhqk,bqhd->bkhd", dscore, query_matrix, preferred_element_type=jnp.float32
    )
    value_term = jnp.einsum(
        "bhqk,bqhd->bkhd", softmax_weights, gradient_rows, preferred_element_type=jnp.float32
    )
    terms = jnp.concatenate(
        [
            key_term.reshape(block_count, key_count, BLOCK_TOKENS, feature_width),
            value_term.reshape(block_count, key_count, BLOCK_TOKENS, feature_width),
        ],
        axis=3,
    )
    zero_one = jnp.zeros((1, BLOCK_TOKENS, double_width), jnp.float32)
    zero_two = jnp.zeros((2, BLOCK_TOKENS, double_width), jnp.float32)
    ext_grad = (
        jnp.concatenate([terms[:, 0], zero_two], axis=0)
        + jnp.concatenate([zero_one, terms[:, 1], zero_one], axis=0)
        + jnp.concatenate([zero_two, terms[:, 2]], axis=0)
    )
    rims = jnp.concatenate([ext_grad[0], ext_grad[-1]], axis=0)
    returned = extended_2(rims, (("seq", 0),), BLOCK_TOKENS)
    own = ext_grad[1:-1]
    own = own.at[0].add(returned[:BLOCK_TOKENS]).at[-1].add(returned[3 * BLOCK_TOKENS :])
    glob_terms = jnp.sum(terms[:, 3:nfixed], axis=0)
    glob_total = lax.psum(glob_terms, "seq")
    block_ids = jnp.arange(block_count)
    for glob_index in range(nglob):
        owned_here = (block_ids == local_glob[glob_index]) & (owners_glob[glob_index] == myself)
        own = own + jnp.where(owned_here[:, None, None], glob_total[glob_index][None], 0.0)
    tile_terms = terms[:, nfixed:].reshape(needed, BLOCK_TOKENS, double_width).astype(jnp.bfloat16)
    empty = jnp.zeros((nshard * slots,) + tile_terms.shape[1:], tile_terms.dtype)
    arrived = lax.all_to_all(
        empty.at[flat_slot].set(tile_terms).reshape((nshard, slots) + tile_terms.shape[1:]),
        "seq",
        split_axis=0,
        concat_axis=0,
        tiled=True,
    )
    selector = (send_local.reshape(-1)[None, :] == block_ids[:, None]) & valid.reshape(-1)[None, :]
    own = own + jnp.einsum(
        "bs,sqc->bqc",
        selector.astype(jnp.bfloat16),
        arrived.reshape(nshard * slots, BLOCK_TOKENS, double_width),
        preferred_element_type=jnp.float32,
    )
    own = own.reshape(tokens, double_width)
    dkey = own[:, :feature_width].astype(jnp.bfloat16)
    dvalue = own[:, feature_width:].astype(jnp.bfloat16)
    return (out, query_gradient, dkey, dvalue)


PAIRS = 4
SIDE = 2 * HEAD_SIZE
MASKED = -1e30
NT = (((1,), (1,)), ((), ()))
TN = (((0,), (0,)), ((), ()))
NN = (((1,), (0,)), ((), ()))


def dot(a, b, dims):
    return lax.dot_general(a, b, dims, preferred_element_type=jnp.float32)


def fused_kernel(
    rand_ref, glob_ref, q_ref, k_ref, v_ref, g_ref,
    o_ref, dq_ref, dk_ref, dv_ref,
    kv, qg, pack, bias, score, dprob, top, total, acc_out, acc_dq,
    part, send, from_near, from_far, swap_out, swap_in,
    far_sent, near_sent, kv_got, grad_sent, near_got, far_got, swap_sent, swap_got,
):
    tokens = q_ref.shape[0]
    rows = 2 * tokens
    blocks = tokens // BLOCK_TOKENS
    nrand = rand_ref.shape[1]
    nglob = glob_ref.shape[0]
    block_total = rand_ref.shape[0]
    scale = 1.0 / math.sqrt(HEAD_SIZE)
    scale2 = scale * math.log2(math.e)

    s = lax.axis_index("seq")
    z, x = s // 2, s % 2
    partner = s + 1 - 2 * x
    m = z // 2
    w = z + m * (3 - 2 * z)
    step = 1 - 2 * m
    far = 2 * (z + step) + x
    near = 2 * (z - step) + x

    def slot_of(k, other):
        return 2 * (k + m * (3 - 2 * k)) + x + other * (1 - 2 * x)

    def remote(src, dst, sent, got, to):
        return pltpu.make_async_remote_copy(
            src_ref=src, dst_ref=dst, send_sem=sent, recv_sem=got,
            device_id={"seq": to}, device_id_type=pl.DeviceIdType.MESH,
        )

    def kv_far(slot):
        return remote(kv.at[slot], kv.at[slot], far_sent.at[slot], kv_got.at[slot], far)

    def kv_near(slot):
        return remote(kv.at[slot], kv.at[slot], near_sent.at[slot], kv_got.at[slot], near)

    kv_swap = remote(pack.at[0], kv.at[s], swap_sent.at[0], kv_got.at[s], partner)
    kv_swapped = remote(pack.at[0], kv.at[partner], swap_sent.at[0], kv_got.at[partner], partner)
    qg_swap = remote(pack.at[1], qg.at[x], swap_sent.at[1], swap_got.at[0], partner)
    oq_swap = remote(swap_out.at[0], swap_in.at[0], swap_sent.at[2], swap_got.at[1], partner)
    kg_swap = remote(swap_out.at[1], swap_in.at[1], swap_sent.at[3], swap_got.at[2], partner)

    barrier = pltpu.get_barrier_semaphore()
    for to in (partner, far):
        pl.semaphore_signal(
            barrier, inc=1, device_id={"seq": to}, device_id_type=pl.DeviceIdType.MESH
        )

    @pl.when(w == 1)
    def _():
        pl.semaphore_signal(
            barrier, inc=1, device_id={"seq": near}, device_id_type=pl.DeviceIdType.MESH
        )

    mine = pl.ds(pl.multiple_of(x * HEAD_SIZE, HEAD_SIZE), HEAD_SIZE)
    theirs = pl.ds(pl.multiple_of((1 - x) * HEAD_SIZE, HEAD_SIZE), HEAD_SIZE)
    kv[s, :, :HEAD_SIZE] = k_ref[:, mine]
    kv[s, :, HEAD_SIZE:] = v_ref[:, mine]
    pack[0, :, :HEAD_SIZE] = k_ref[:, theirs]
    pack[0, :, HEAD_SIZE:] = v_ref[:, theirs]
    qg[x, :, :HEAD_SIZE] = q_ref[:, mine]
    qg[x, :, HEAD_SIZE:] = g_ref[:, mine]
    pack[1, :, :HEAD_SIZE] = q_ref[:, theirs]
    pack[1, :, HEAD_SIZE:] = g_ref[:, theirs]

    pl.semaphore_wait(barrier, 2 + w)
    kv_swap.start()
    kv_far(s).start()

    @pl.when(w == 1)
    def _():
        kv_near(s).start()

    qg_swap.start()

    lane_block = lax.broadcasted_iota(jnp.int32, (1, rows), 1) // BLOCK_TOKENS
    first = z * 2 * blocks
    block = first + lane_block
    entries = [
        jnp.where(block == 0, block_total - 1, block - 1),
        block,
        jnp.where(block == block_total - 1, 0, block + 1),
    ]
    for j in range(nglob):
        entries.append(jnp.full((1, rows), glob_ref[j], jnp.int32))
    for j in range(nrand):
        entry = jnp.zeros((1, rows), jnp.int32)
        for i in range(2 * blocks):
            entry = jnp.where(lane_block == i, rand_ref[first + i, j], entry)
        entries.append(entry)
    key_block = lax.broadcasted_iota(jnp.int32, (block_total, rows), 0)
    count = jnp.zeros((block_total, rows), jnp.float32)
    for entry in entries:
        count = count + jnp.where(key_block == entry, 1.0, 0.0)
    bias_all = jnp.where(count > 0.0, jnp.log2(jnp.maximum(count, 1.0)), MASKED)
    for j in range(2 * PAIRS):
        bias[j] = bias_all[j * blocks : (j + 1) * blocks]

    top[...] = jnp.full_like(top, MASKED)
    total[...] = jnp.zeros_like(total)
    acc_out[...] = jnp.zeros_like(acc_out)
    acc_dq[...] = jnp.zeros_like(acc_dq)

    kv_swapped.wait_recv()
    kv_far(partner).start()

    @pl.when(w == 1)
    def _():
        kv_near(partner).start()

    qg_swap.wait_recv()

    def queries():
        return qg[:, :, :HEAD_SIZE].reshape(rows, HEAD_SIZE)

    def grads():
        return qg[:, :, HEAD_SIZE:].reshape(rows, HEAD_SIZE)

    def forward(slot):
        key = kv[slot, :, :HEAD_SIZE]
        value = kv[slot, :, HEAD_SIZE:]
        st = dot(key, queries(), NT) * scale2
        st = (st.reshape(blocks, BLOCK_TOKENS, rows) + bias[slot][:, None, :]).reshape(tokens, rows)
        score[slot] = st
        old = top[...]
        new = jnp.maximum(old, jnp.max(st, axis=0, keepdims=True))
        e = jnp.exp2(st - new)
        alpha = jnp.exp2(old - new)
        top[...] = new
        total[...] = total[...] * alpha + jnp.sum(e, axis=0, keepdims=True)
        acc_out[...] = acc_out[...] * alpha + dot(value, e.astype(jnp.bfloat16), TN)
        dprob[slot] = dot(value, grads(), NT)

    @pl.loop(0, 2)
    def _(i):
        forward(s + i * (1 - 2 * x))

    @pl.loop(0, 6)
    def _(i):
        k_end = 1 + i // 2
        o_end = i % 2
        k_mid = jnp.where(i < 4, (i % 2) * 2, 3)
        o_mid = jnp.where(i < 4, i // 2, i % 2)
        k = jnp.where(w == 0, k_end, k_mid)
        slot = slot_of(k, jnp.where(w == 0, o_end, o_mid))
        kv_far(slot).wait_recv()

        @pl.when((w == 1) & (k == 0))
        def _():
            kv_far(slot).start()

        @pl.when((w == 1) & (k > 0))
        def _():
            kv_near(slot).start()

        forward(slot)

    lse = top[...] + jnp.log2(total[...])
    out_t = (acc_out[...] / total[...]).astype(jnp.bfloat16).astype(jnp.float32)
    grad_t = grads().astype(jnp.float32).T
    delta = jnp.sum(out_t * grad_t, axis=0, keepdims=True)
    acc_out[...] = out_t
    top[...] = lse
    total[...] = delta

    def grad_send(slot, to, got, sem):
        return remote(send.at[slot], got.at[slot], grad_sent.at[slot], sem.at[slot], to)

    @pl.loop(0, 8)
    def _(i):
        k_low = jnp.where(w == 0, 3 - i // 2, i // 2 - 2)
        k = jnp.where(i < 4, 3 - i // 2, k_low)
        slot = slot_of(k, 1 - i % 2)
        prob = jnp.exp2(score[slot] - top[...])
        ds = (prob * (dprob[slot] - total[...]) * scale).astype(jnp.bfloat16)
        dk_term = dot(ds, queries(), NN)
        dv_term = dot(prob.astype(jnp.bfloat16), grads(), NN)
        is_sent = (w == 0) & (i < 6)

        @pl.when(is_sent)
        def _():
            send[slot, :, :HEAD_SIZE] = dk_term.astype(jnp.bfloat16)
            send[slot, :, HEAD_SIZE:] = dv_term.astype(jnp.bfloat16)
            grad_send(slot, far, from_near, near_got).start()

        @pl.when(jnp.logical_not(is_sent))
        def _():
            part[slot, :, :HEAD_SIZE] = dk_term
            part[slot, :, HEAD_SIZE:] = dv_term

        acc_dq[...] += dot(kv[slot, :, :HEAD_SIZE], ds, TN)

    out_rows = acc_out[...].T.astype(jnp.bfloat16)
    dq_rows = acc_dq[...].T.astype(jnp.bfloat16)
    low_o, high_o = out_rows[:tokens], out_rows[tokens:]
    low_q, high_q = dq_rows[:tokens], dq_rows[tokens:]

    @pl.when(x == 0)
    def _():
        swap_out[0, :, :HEAD_SIZE] = high_o
        swap_out[0, :, HEAD_SIZE:] = high_q
        o_ref[:, :HEAD_SIZE] = low_o
        dq_ref[:, :HEAD_SIZE] = low_q

    @pl.when(x == 1)
    def _():
        swap_out[0, :, :HEAD_SIZE] = low_o
        swap_out[0, :, HEAD_SIZE:] = low_q
        o_ref[:, HEAD_SIZE:] = high_o
        dq_ref[:, HEAD_SIZE:] = high_q

    oq_swap.start()

    @pl.when(w == 1)
    def _():
        for k, other in ((3, 1), (3, 0), (0, 1), (2, 1), (0, 0), (2, 0)):
            slot = slot_of(k, other)
            if k == 0:
                grad_send(slot, far, from_far, far_got).wait_recv()
                added = part[slot] + from_far[slot].astype(jnp.float32)
                send[slot] = added.astype(jnp.bfloat16)
                grad_send(slot, near, from_far, far_got).start()
            else:
                grad_send(slot, far, from_near, near_got).wait_recv()
                added = part[slot] + from_near[slot].astype(jnp.float32)
                send[slot] = added.astype(jnp.bfloat16)
                grad_send(slot, far, from_far, far_got).start()

    def finish(slot):
        grad_send(slot, far, from_far, far_got).wait_recv()
        part[slot] += from_far[slot].astype(jnp.float32)

        @pl.when(w == 1)
        def _():
            grad_send(slot, far, from_near, near_got).wait_recv()
            part[slot] += from_near[slot].astype(jnp.float32)

    finish(partner)
    swap_out[1] = part[partner].astype(jnp.bfloat16)
    kg_swap.start()
    finish(s)
    dk_ref[:, mine] = part[s, :, :HEAD_SIZE].astype(jnp.bfloat16)
    dv_ref[:, mine] = part[s, :, HEAD_SIZE:].astype(jnp.bfloat16)
    oq_swap.wait_recv()
    o_ref[:, theirs] = swap_in[0, :, :HEAD_SIZE]
    dq_ref[:, theirs] = swap_in[0, :, HEAD_SIZE:]

    kv_swap.wait_send()
    qg_swap.wait_send()
    oq_swap.wait_send()
    for slot in (s, partner):
        kv_far(slot).wait_send()

    @pl.when(w == 0)
    def _():
        for k in (1, 2, 3):
            for other in (0, 1):
                grad_send(slot_of(k, other), far, from_near, near_got).wait_send()

    @pl.when(w == 1)
    def _():
        for other in (0, 1):
            kv_far(slot_of(0, other)).wait_send()
            for k in (1, 2, 3):
                kv_near(slot_of(k, other)).wait_send()
            for k in (0, 2, 3):
                grad_send(slot_of(k, other), far, from_far, far_got).wait_send()

    kg_swap.wait_recv()
    dk_ref[:, theirs] = swap_in[1, :, :HEAD_SIZE]
    dv_ref[:, theirs] = swap_in[1, :, HEAD_SIZE:]
    kg_swap.wait_send()


def fused(query, key_states, values, grad_out, rand_blocks, global_blocks):
    tokens = query.shape[0]
    rows = 2 * tokens
    slots = 2 * PAIRS
    blocks = tokens // BLOCK_TOKENS
    bf16, f32 = jnp.bfloat16, jnp.float32
    vmem = pl.BlockSpec(memory_space=pltpu.VMEM)
    smem = pl.BlockSpec(memory_space=pltpu.SMEM)
    dma = pltpu.SemaphoreType.DMA
    work = 6 * 2 * rows * slots * tokens * HEAD_SIZE
    return pl.pallas_call(
        fused_kernel,
        out_shape=[jax.ShapeDtypeStruct(query.shape, bf16)] * 4,
        in_specs=[smem, smem, vmem, vmem, vmem, vmem],
        out_specs=[vmem] * 4,
        scratch_shapes=[
            pltpu.VMEM((slots, tokens, SIDE), bf16),
            pltpu.VMEM((2, tokens, SIDE), bf16),
            pltpu.VMEM((2, tokens, SIDE), bf16),
            pltpu.VMEM((slots, blocks, rows), f32),
            pltpu.VMEM((slots, tokens, rows), f32),
            pltpu.VMEM((slots, tokens, rows), f32),
            pltpu.VMEM((1, rows), f32),
            pltpu.VMEM((1, rows), f32),
            pltpu.VMEM((HEAD_SIZE, rows), f32),
            pltpu.VMEM((HEAD_SIZE, rows), f32),
            pltpu.VMEM((slots, tokens, SIDE), f32),
            pltpu.VMEM((slots, tokens, SIDE), bf16),
            pltpu.VMEM((slots, tokens, SIDE), bf16),
            pltpu.VMEM((slots, tokens, SIDE), bf16),
            pltpu.VMEM((2, tokens, SIDE), bf16),
            pltpu.VMEM((2, tokens, SIDE), bf16),
            dma((slots,)), dma((slots,)), dma((slots,)), dma((slots,)),
            dma((slots,)), dma((slots,)), dma((4,)), dma((3,)),
        ],
        compiler_params=pltpu.CompilerParams(
            collective_id=0, has_side_effects=True, vmem_limit_bytes=40 * 1024 * 1024
        ),
        cost_estimate=pl.CostEstimate(
            flops=work, bytes_accessed=8 * tokens * SIDE * 2, transcendentals=2 * rows * slots * tokens
        ),
    )(rand_blocks, global_blocks, query, key_states, values, grad_out)


def device_program(query, key_states, values, grad_out, rand_blocks, global_blocks):
    if lax.axis_size("seq") == 2 * PAIRS and query.shape == (4 * BLOCK_TOKENS, 2 * HEAD_SIZE):
        return tuple(fused(query, key_states, values, grad_out, rand_blocks, global_blocks))
    return shards(query, key_states, values, grad_out, rand_blocks, global_blocks)


def solution(mesh):
    in_specs = (P("seq", "head"), P("seq", "head"), P("seq", "head"), P("seq", "head"), P(), P())
    out_specs = (P("seq", "head"), P("seq", "head"), P("seq", "head"), P("seq", "head"))
    return jax.shard_map(
        device_program, mesh=mesh, in_specs=in_specs, out_specs=out_specs, check_vma=False
    )
```

```python
import math

import jax
import jax.numpy as jnp
from jax import lax
from jax.experimental import pallas as pl
from jax.experimental.pallas import tpu as pltpu
from jax.sharding import PartitionSpec as P

HEAD_SIZE = 128
BLOCK_TOKENS = 64


def extended_2(block, sides, width):
    for axis, dim in sides:
        count = lax.axis_size(axis)
        forward = [(i, i + 1) for i in range(count - 1)]
        forward.append((count - 1, 0))
        backward = [(target, source) for source, target in forward]
        low = lax.ppermute(
            lax.slice_in_dim(block, block.shape[dim] - width, None, axis=dim), axis, forward
        )
        high = lax.ppermute(lax.slice_in_dim(block, 0, width, axis=dim), axis, backward)
        block = jnp.concatenate([low, block, high], axis=dim)
    return block


def pick_blocks(blocks, index):
    onehot = (index[..., None] == jnp.arange(blocks.shape[0])).astype(blocks.dtype)
    picked = jnp.einsum(
        "...b,bqc->...qc", onehot, blocks, preferred_element_type=jnp.float32
    )
    return picked.astype(blocks.dtype)


def shards(query, key_states, values, grad_out, rand_blocks, global_blocks):
    tokens, feature_width = query.shape
    head_count = feature_width // HEAD_SIZE
    nshard = lax.axis_size("seq")
    myself = lax.axis_index("seq")
    block_count = tokens // BLOCK_TOKENS
    nrand = rand_blocks.shape[1]
    nglob = global_blocks.shape[0]
    nfixed = 3 + nglob
    needed = block_count * nrand
    slots = max(2, (needed + nshard - 1) // nshard)
    double_width = 2 * feature_width
    score_scale = 1.0 / math.sqrt(HEAD_SIZE)
    paired = jnp.concatenate([key_states, values], axis=1)
    paired_blocks = paired.reshape(block_count, BLOCK_TOKENS, double_width)
    extended = extended_2(paired, (("seq", 0),), BLOCK_TOKENS)
    owners_glob = global_blocks // block_count
    local_glob = global_blocks % block_count
    pieces = []
    for glob_index in range(nglob):
        piece = lax.dynamic_slice_in_dim(
            paired, local_glob[glob_index] * BLOCK_TOKENS, BLOCK_TOKENS, 0
        )
        pieces.append(jnp.where(owners_glob[glob_index] == myself, piece.astype(jnp.float32), 0.0))
    global_rows = lax.psum(jnp.concatenate(pieces, axis=0), "seq").astype(jnp.bfloat16)
    table = rand_blocks.reshape(nshard, needed)
    owner_table = table // block_count
    local_table = table % block_count
    position = jnp.arange(needed)
    earlier_same = (owner_table[:, :, None] == owner_table[:, None, :]) & (
        position[None, None, :] < position[None, :, None]
    )
    rank_table = jnp.sum(earlier_same.astype(jnp.int32), axis=2)
    slot_range = jnp.arange(slots)
    matched = (owner_table[:, :, None] == myself) & (
        rank_table[:, :, None] == slot_range[None, None, :]
    )
    valid = jnp.any(matched, axis=1)
    send_local = jnp.sum(jnp.where(matched, local_table[:, :, None], 0), axis=1)
    outgoing = jnp.where(
        valid[:, :, None, None], pick_blocks(paired_blocks, send_local), jnp.zeros((), jnp.bfloat16)
    )
    incoming = lax.all_to_all(outgoing, "seq", split_axis=0, concat_axis=0, tiled=True)
    my_owner = lax.dynamic_index_in_dim(owner_table, myself, 0, keepdims=False)
    my_rank = lax.dynamic_index_in_dim(rank_table, myself, 0, keepdims=False)
    flat_slot = my_owner * slots + my_rank
    fetched = pick_blocks(
        incoming.reshape(nshard * slots, BLOCK_TOKENS, double_width), flat_slot
    ).reshape(block_count, nrand, BLOCK_TOKENS, double_width)
    ext_blocks = extended.reshape(block_count + 2, BLOCK_TOKENS, double_width)
    window_blocks = jnp.stack([ext_blocks[:-2], ext_blocks[1:-1], ext_blocks[2:]], axis=1)
    glob_wide = jnp.broadcast_to(
        global_rows.reshape(1, nglob, BLOCK_TOKENS, double_width),
        (block_count, nglob, BLOCK_TOKENS, double_width),
    )
    gathered = jnp.concatenate([window_blocks, glob_wide, fetched], axis=1)
    key_count = gathered.shape[1]
    key_matrix = gathered[..., :feature_width].reshape(
        block_count, key_count * BLOCK_TOKENS, head_count, HEAD_SIZE
    )
    value_matrix = gathered[..., feature_width:].reshape(
        block_count, key_count * BLOCK_TOKENS, head_count, HEAD_SIZE
    )
    query_matrix = query.reshape(block_count, BLOCK_TOKENS, head_count, HEAD_SIZE)
    logit_scores = (
        jnp.einsum("bqhd,bkhd->bhqk", query_matrix, key_matrix, preferred_element_type=jnp.float32)
        * score_scale
    )
    top = jnp.max(logit_scores, axis=-1, keepdims=True)
    lse = top + jnp.log(jnp.sum(jnp.exp(logit_scores - top), axis=-1, keepdims=True))
    probs = jnp.exp(logit_scores - lse)
    softmax_weights = probs.astype(jnp.bfloat16)
    attended_output = jnp.einsum(
        "bhqk,bkhd->bqhd", softmax_weights, value_matrix, preferred_element_type=jnp.float32
    ).astype(jnp.bfloat16)
    out = attended_output.reshape(tokens, feature_width)
    gradient_rows = grad_out.reshape(block_count, BLOCK_TOKENS, head_count, HEAD_SIZE)
    delta = jnp.sum(gradient_rows.astype(jnp.float32) * attended_output.astype(jnp.float32), axis=3)
    delta = jnp.transpose(delta, (0, 2, 1))[..., None]
    probability_gradient = jnp.einsum(
        "bqhd,bkhd->bhqk", gradient_rows, value_matrix, preferred_element_type=jnp.float32
    )
    dscore = (probs * (probability_gradient - delta) * score_scale).astype(jnp.bfloat16)
    query_gradient = jnp.einsum(
        "bhqk,bkhd->bqhd", dscore, key_matrix, preferred_element_type=jnp.float32
    ).astype(jnp.bfloat16)
    query_gradient = query_gradient.reshape(tokens, feature_width)
    key_term = jnp.einsum(
        "bhqk,bqhd->bkhd", dscore, query_matrix, preferred_element_type=jnp.float32
    )
    value_term = jnp.einsum(
        "bhqk,bqhd->bkhd", softmax_weights, gradient_rows, preferred_element_type=jnp.float32
    )
    terms = jnp.concatenate(
        [
            key_term.reshape(block_count, key_count, BLOCK_TOKENS, feature_width),
            value_term.reshape(block_count, key_count, BLOCK_TOKENS, feature_width),
        ],
        axis=3,
    )
    zero_one = jnp.zeros((1, BLOCK_TOKENS, double_width), jnp.float32)
    zero_two = jnp.zeros((2, BLOCK_TOKENS, double_width), jnp.float32)
    ext_grad = (
        jnp.concatenate([terms[:, 0], zero_two], axis=0)
        + jnp.concatenate([zero_one, terms[:, 1], zero_one], axis=0)
        + jnp.concatenate([zero_two, terms[:, 2]], axis=0)
    )
    rims = jnp.concatenate([ext_grad[0], ext_grad[-1]], axis=0)
    returned = extended_2(rims, (("seq", 0),), BLOCK_TOKENS)
    own = ext_grad[1:-1]
    own = own.at[0].add(returned[:BLOCK_TOKENS]).at[-1].add(returned[3 * BLOCK_TOKENS :])
    glob_terms = jnp.sum(terms[:, 3:nfixed], axis=0)
    glob_total = lax.psum(glob_terms, "seq")
    block_ids = jnp.arange(block_count)
    for glob_index in range(nglob):
        owned_here = (block_ids == local_glob[glob_index]) & (owners_glob[glob_index] == myself)
        own = own + jnp.where(owned_here[:, None, None], glob_total[glob_index][None], 0.0)
    tile_terms = terms[:, nfixed:].reshape(needed, BLOCK_TOKENS, double_width).astype(jnp.bfloat16)
    empty = jnp.zeros((nshard * slots,) + tile_terms.shape[1:], tile_terms.dtype)
    arrived = lax.all_to_all(
        empty.at[flat_slot].set(tile_terms).reshape((nshard, slots) + tile_terms.shape[1:]),
        "seq",
        split_axis=0,
        concat_axis=0,
        tiled=True,
    )
    selector = (send_local.reshape(-1)[None, :] == block_ids[:, None]) & valid.reshape(-1)[None, :]
    own = own + jnp.einsum(
        "bs,sqc->bqc",
        selector.astype(jnp.bfloat16),
        arrived.reshape(nshard * slots, BLOCK_TOKENS, double_width),
        preferred_element_type=jnp.float32,
    )
    own = own.reshape(tokens, double_width)
    dkey = own[:, :feature_width].astype(jnp.bfloat16)
    dvalue = own[:, feature_width:].astype(jnp.bfloat16)
    return (out, query_gradient, dkey, dvalue)


PAIRS = 4
SIDE = 2 * HEAD_SIZE
MASKED = -1e30
NT = (((1,), (1,)), ((), ()))
TN = (((0,), (0,)), ((), ()))
NN = (((1,), (0,)), ((), ()))


def dot(a, b, dims):
    return lax.dot_general(a, b, dims, preferred_element_type=jnp.float32)


def fused_kernel(
    rand_ref, glob_ref, q_ref, k_ref, v_ref, g_ref,
    res_ref,
    kv, own, qg, pack, bias, score, dprob, top, total, acc_out, acc_dq,
    part, cross, cross_in, line, line_in, swap_out, swap_in,
    loaded, line_sent, cross_sent, kv_got, swap_sent, swap_got,
    grad_cross_sent, grad_cross_got, grad_line_sent, grad_line_got,
):
    tokens = q_ref.shape[0]
    rows = 2 * tokens
    blocks = tokens // BLOCK_TOKENS
    nrand = rand_ref.shape[0]
    nglob = glob_ref.shape[0]
    block_total = rand_ref.shape[1]
    scale = 1.0 / math.sqrt(HEAD_SIZE)
    scale2 = scale * math.log2(math.e)

    s = lax.axis_index("seq")
    z, x = s // 2, s % 2
    partner = s + 1 - 2 * x
    zq = z % 2
    mate = z + 1 - 2 * zq
    skip = (z + 2) % PAIRS
    mirror = PAIRS - 1 - z
    head = ((z + 1) // 2) % 2
    tour = (skip, mirror, mate)

    def remote(src, dst, sent, got, to):
        return pltpu.make_async_remote_copy(
            src_ref=src, dst_ref=dst, send_sem=sent, recv_sem=got,
            device_id={"seq": to}, device_id_type=pl.DeviceIdType.MESH,
        )

    def kv_line(zz):
        their_head = ((zz + 1) // 2) % 2
        return remote(own.at[their_head], kv.at[s], line_sent.at[zz], kv_got.at[s], 2 * zz + x)

    def kv_cross(zz):
        slot = 2 * zz + x
        return remote(kv.at[slot], kv.at[slot], cross_sent.at[zz], kv_got.at[slot], partner)

    def kv_arrival(slot):
        return remote(kv.at[slot], kv.at[slot], cross_sent.at[0], kv_got.at[slot], partner)

    to_mate = 2 * mate + x
    qg_swap = remote(pack, qg.at[zq], swap_sent.at[0], swap_got.at[0], to_mate)
    o_swap = remote(swap_out.at[0], swap_in.at[0], swap_sent.at[1], swap_got.at[1], to_mate)
    q_swap = remote(swap_out.at[1], swap_in.at[1], swap_sent.at[2], swap_got.at[2], to_mate)

    def grad_cross(zz):
        return remote(
            cross.at[zz], cross_in.at[zz], grad_cross_sent.at[zz], grad_cross_got.at[zz], partner
        )

    def grad_line(zz):
        return remote(
            line.at[zz], line_in.at[z], grad_line_sent.at[zz], grad_line_got.at[z], 2 * zz + x
        )

    def grad_arrival(zz):
        return remote(
            line.at[zz], line_in.at[zz], grad_line_sent.at[zz], grad_line_got.at[zz], 2 * zz + x
        )

    mine = pl.ds(pl.multiple_of(head * HEAD_SIZE, HEAD_SIZE), HEAD_SIZE)
    theirs = pl.ds(pl.multiple_of((1 - head) * HEAD_SIZE, HEAD_SIZE), HEAD_SIZE)
    low, high = pl.ds(0, HEAD_SIZE), pl.ds(HEAD_SIZE, HEAD_SIZE)
    loads = []
    for src, lanes, dst in (
        (q_ref, theirs, pack.at[:, low]), (g_ref, theirs, pack.at[:, high]),
        (k_ref, low, own.at[0, :, low]), (v_ref, low, own.at[0, :, high]),
        (k_ref, high, own.at[1, :, low]), (v_ref, high, own.at[1, :, high]),
        (k_ref, mine, kv.at[s, :, low]), (v_ref, mine, kv.at[s, :, high]),
        (q_ref, mine, qg.at[zq, :, low]), (g_ref, mine, qg.at[zq, :, high]),
    ):
        loads.append(pltpu.make_async_copy(src.at[:, lanes], dst, loaded.at[len(loads)]))
        loads[-1].start()

    barrier = pltpu.get_barrier_semaphore()
    for to in (partner, to_mate, 2 * skip + x, 2 * mirror + x):
        pl.semaphore_signal(
            barrier, inc=1, device_id={"seq": to}, device_id_type=pl.DeviceIdType.MESH
        )
    pl.semaphore_wait(barrier, 4)
    loads[0].wait()
    loads[1].wait()
    qg_swap.start()
    for load in loads[2:8]:
        load.wait()
    kv_cross(z).start()
    for zz in tour:
        kv_line(zz).start()

    lane_shard = lax.broadcasted_iota(jnp.int32, (1, rows), 1) // tokens
    lane_block = lax.broadcasted_iota(jnp.int32, (1, rows), 1) // BLOCK_TOKENS
    base = 4 * (z // 2) + x
    block = (base + 2 * lane_shard) * blocks + lane_block - lane_shard * blocks
    entries = [
        jnp.where(block == 0, block_total - 1, block - 1),
        block,
        jnp.where(block == block_total - 1, 0, block + 1),
    ]
    for j in range(nglob):
        entries.append(jnp.full((1, rows), glob_ref[j], jnp.int32))
    for j in range(nrand):
        entry = jnp.zeros((1, rows), jnp.int32)
        for i in range(2 * blocks):
            there = (base + 2 * (i // blocks)) * blocks + i % blocks
            entry = jnp.where(lane_block == i, rand_ref[j, there], entry)
        entries.append(entry)
    key_block = lax.broadcasted_iota(jnp.int32, (block_total, rows), 0)
    count = jnp.zeros((block_total, rows), jnp.float32)
    for entry in entries:
        count = count + jnp.where(key_block == entry, 1.0, 0.0)
    bias_all = jnp.where(count > 0.0, jnp.log2(jnp.maximum(count, 1.0)), MASKED)
    for j in range(2 * PAIRS):
        bias[j] = bias_all[j * blocks : (j + 1) * blocks]

    top[...] = jnp.full_like(top, MASKED)
    total[...] = jnp.zeros_like(total)
    acc_out[...] = jnp.zeros_like(acc_out)
    acc_dq[...] = jnp.zeros_like(acc_dq)
    loads[8].wait()
    loads[9].wait()
    remote(pack, qg.at[1 - zq], swap_sent.at[0], swap_got.at[0], to_mate).wait_recv()

    def queries():
        return qg[:, :, :HEAD_SIZE].reshape(rows, HEAD_SIZE)

    def grads():
        return qg[:, :, HEAD_SIZE:].reshape(rows, HEAD_SIZE)

    def tour_at(i):
        return jnp.where(i == 0, skip, jnp.where(i == 1, mirror, jnp.where(i == 2, mate, z)))

    def forward(slot):
        key = kv[slot, :, :HEAD_SIZE]
        value = kv[slot, :, HEAD_SIZE:]
        st = dot(key, queries(), NT) * scale2
        st = (st.reshape(blocks, BLOCK_TOKENS, rows) + bias[slot][:, None, :]).reshape(tokens, rows)
        score[slot] = st
        old = top[...]
        new = jnp.maximum(old, jnp.max(st, axis=0, keepdims=True))
        e = jnp.exp2(st - new)
        alpha = jnp.exp2(old - new)
        top[...] = new
        total[...] = total[...] * alpha + jnp.sum(e, axis=0, keepdims=True)
        acc_out[...] = acc_out[...] * alpha + dot(value, e.astype(jnp.bfloat16), TN)
        dprob[slot] = dot(value, grads(), NT)

    @pl.loop(0, 8)
    def _(i):
        zz = jnp.where(i < 2, z, tour_at((i - 2) % 3))
        column = jnp.where((i == 1) | (i > 4), 1 - x, x)
        slot = 2 * zz + column

        @pl.when(i > 0)
        def _():
            kv_arrival(slot).wait_recv()

        @pl.when((i >= 2) & (i <= 4))
        def _():
            kv_cross(zz).start()

        forward(slot)

    lse = top[...] + jnp.log2(total[...])
    out_t = (acc_out[...] / total[...]).astype(jnp.bfloat16).astype(jnp.float32)
    grad_t = grads().astype(jnp.float32).T
    delta = jnp.sum(out_t * grad_t, axis=0, keepdims=True)
    acc_out[...] = out_t
    top[...] = lse
    total[...] = delta

    def backward(slot):
        prob = jnp.exp2(score[slot] - top[...])
        ds = (prob * (dprob[slot] - total[...]) * scale).astype(jnp.bfloat16)
        dk_term = dot(ds, queries(), NN)
        dv_term = dot(prob.astype(jnp.bfloat16), grads(), NN)
        return ds, dk_term, dv_term

    def add_dq(slot, ds):
        acc_dq[...] += dot(kv[slot, :, :HEAD_SIZE], ds, TN)

    @pl.loop(0, 4)
    def _(i):
        zz = tour_at(i)
        slot = 2 * zz + 1 - x
        ds, dk_term, dv_term = backward(slot)
        cross[zz, :, :HEAD_SIZE] = dk_term.astype(jnp.bfloat16)
        cross[zz, :, HEAD_SIZE:] = dv_term.astype(jnp.bfloat16)
        grad_cross(zz).start()
        add_dq(slot, ds)

    def hand_back(which, rows_t, swap):
        turned = rows_t.T.astype(jnp.bfloat16)
        first, second = turned[:tokens], turned[tokens:]
        swap_out[which] = jnp.where(zq == 0, second, first)
        res_ref[which, :, mine] = jnp.where(zq == 0, first, second)
        swap.start()

    hand_back(0, acc_out[...], o_swap)

    @pl.loop(0, 4)
    def _(i):
        zz = tour_at(i)
        slot = 2 * zz + x
        ds, dk_term, dv_term = backward(slot)
        part[zz, :, :HEAD_SIZE] = dk_term
        part[zz, :, HEAD_SIZE:] = dv_term
        add_dq(slot, ds)

        @pl.when(i < 3)
        def _():
            grad_cross(zz).wait_recv()
            added = part[zz] + cross_in[zz].astype(jnp.float32)
            line[zz] = added.astype(jnp.bfloat16)
            grad_line(zz).start()

    hand_back(1, acc_dq[...], q_swap)

    grad_cross(z).wait_recv()
    grad_arrival(mirror).wait_recv()
    same = part[z] + cross_in[z].astype(jnp.float32) + line_in[mirror].astype(jnp.float32)
    res_ref[2, :, mine] = same[:, :HEAD_SIZE].astype(jnp.bfloat16)
    res_ref[3, :, mine] = same[:, HEAD_SIZE:].astype(jnp.bfloat16)

    qg_swap.wait_send()
    kv_cross(z).wait_send()
    for zz in tour:
        kv_line(zz).wait_send()
        kv_cross(zz).wait_send()
    o_swap.wait()
    res_ref[0, :, theirs] = swap_in[0]
    q_swap.wait()
    res_ref[1, :, theirs] = swap_in[1]
    grad_arrival(skip).wait_recv()
    grad_arrival(mate).wait_recv()
    other = line_in[skip].astype(jnp.float32) + line_in[mate].astype(jnp.float32)
    res_ref[2, :, theirs] = other[:, :HEAD_SIZE].astype(jnp.bfloat16)
    res_ref[3, :, theirs] = other[:, HEAD_SIZE:].astype(jnp.bfloat16)
    for zz in tour:
        grad_cross(zz).wait_send()
        grad_line(zz).wait_send()
    grad_cross(z).wait_send()


def split_kernel(res_ref, o_ref, dq_ref, dk_ref, dv_ref, sems):
    copies = [
        pltpu.make_async_copy(res_ref.at[i], dst, sems.at[i])
        for i, dst in enumerate((o_ref, dq_ref, dk_ref, dv_ref))
    ]
    for copy in copies:
        copy.start()
    for copy in copies:
        copy.wait()


def fused(query, key_states, values, grad_out, rand_blocks, global_blocks):
    tokens = query.shape[0]
    rows = 2 * tokens
    slots = 2 * PAIRS
    blocks = tokens // BLOCK_TOKENS
    bf16, f32 = jnp.bfloat16, jnp.float32
    vmem = pl.BlockSpec(memory_space=pltpu.VMEM)
    smem = pl.BlockSpec(memory_space=pltpu.SMEM)
    hbm = pl.BlockSpec(memory_space=pl.ANY)
    dma = pltpu.SemaphoreType.DMA
    work = 6 * 2 * rows * slots * tokens * HEAD_SIZE
    piece = (tokens, SIDE)
    results = pl.pallas_call(
        fused_kernel,
        out_shape=jax.ShapeDtypeStruct((4,) + query.shape, bf16),
        in_specs=[smem, smem, hbm, hbm, hbm, hbm],
        out_specs=vmem,
        scratch_shapes=[
            pltpu.VMEM((slots,) + piece, bf16),
            pltpu.VMEM((2,) + piece, bf16),
            pltpu.VMEM((2,) + piece, bf16),
            pltpu.VMEM(piece, bf16),
            pltpu.VMEM((slots, blocks, rows), f32),
            pltpu.VMEM((slots, tokens, rows), f32),
            pltpu.VMEM((slots, tokens, rows), f32),
            pltpu.VMEM((1, rows), f32),
            pltpu.VMEM((1, rows), f32),
            pltpu.VMEM((HEAD_SIZE, rows), f32),
            pltpu.VMEM((HEAD_SIZE, rows), f32),
            pltpu.VMEM((PAIRS,) + piece, f32),
            pltpu.VMEM((PAIRS,) + piece, bf16),
            pltpu.VMEM((PAIRS,) + piece, bf16),
            pltpu.VMEM((PAIRS,) + piece, bf16),
            pltpu.VMEM((PAIRS,) + piece, bf16),
            pltpu.VMEM((2, tokens, HEAD_SIZE), bf16),
            pltpu.VMEM((2, tokens, HEAD_SIZE), bf16),
            dma((10,)), dma((PAIRS,)), dma((PAIRS,)), dma((slots,)), dma((3,)), dma((3,)),
            dma((PAIRS,)), dma((PAIRS,)), dma((PAIRS,)), dma((PAIRS,)),
        ],
        compiler_params=pltpu.CompilerParams(
            collective_id=0, has_side_effects=True, vmem_limit_bytes=60 * 1024 * 1024
        ),
        cost_estimate=pl.CostEstimate(
            flops=work, bytes_accessed=8 * tokens * SIDE * 2, transcendentals=2 * rows * slots * tokens
        ),
    )(rand_blocks.T, global_blocks, query, key_states, values, grad_out)
    anywhere = pl.BlockSpec(memory_space=pl.ANY)
    return pl.pallas_call(
        split_kernel,
        out_shape=[jax.ShapeDtypeStruct(query.shape, bf16)] * 4,
        in_specs=[anywhere],
        out_specs=[hbm] * 4,
        scratch_shapes=[dma((4,))],
        cost_estimate=pl.CostEstimate(
            flops=0, bytes_accessed=16 * tokens * SIDE, transcendentals=0
        ),
    )(results)


def device_program(query, key_states, values, grad_out, rand_blocks, global_blocks):
    if lax.axis_size("seq") == 2 * PAIRS and query.shape == (4 * BLOCK_TOKENS, 2 * HEAD_SIZE):
        return tuple(fused(query, key_states, values, grad_out, rand_blocks, global_blocks))
    return shards(query, key_states, values, grad_out, rand_blocks, global_blocks)


def solution(mesh):
    in_specs = (P("seq", "head"), P("seq", "head"), P("seq", "head"), P("seq", "head"), P(), P())
    out_specs = (P("seq", "head"), P("seq", "head"), P("seq", "head"), P("seq", "head"))
    return jax.shard_map(
        device_program, mesh=mesh, in_specs=in_specs, out_specs=out_specs, check_vma=False
    )
```

```python
import math

import jax
import jax.numpy as jnp
from jax import lax
from jax.experimental import pallas as pl
from jax.experimental.pallas import tpu as pltpu
from jax.sharding import PartitionSpec as P

HEAD_SIZE = 128
BLOCK_TOKENS = 64


def extended_2(block, sides, width):
    for axis, dim in sides:
        count = lax.axis_size(axis)
        forward = [(i, i + 1) for i in range(count - 1)]
        forward.append((count - 1, 0))
        backward = [(target, source) for source, target in forward]
        low = lax.ppermute(
            lax.slice_in_dim(block, block.shape[dim] - width, None, axis=dim), axis, forward
        )
        high = lax.ppermute(lax.slice_in_dim(block, 0, width, axis=dim), axis, backward)
        block = jnp.concatenate([low, block, high], axis=dim)
    return block


def pick_blocks(blocks, index):
    onehot = (index[..., None] == jnp.arange(blocks.shape[0])).astype(blocks.dtype)
    picked = jnp.einsum(
        "...b,bqc->...qc", onehot, blocks, preferred_element_type=jnp.float32
    )
    return picked.astype(blocks.dtype)


def shards(query, key_states, values, grad_out, rand_blocks, global_blocks):
    tokens, feature_width = query.shape
    head_count = feature_width // HEAD_SIZE
    nshard = lax.axis_size("seq")
    myself = lax.axis_index("seq")
    block_count = tokens // BLOCK_TOKENS
    nrand = rand_blocks.shape[1]
    nglob = global_blocks.shape[0]
    nfixed = 3 + nglob
    needed = block_count * nrand
    slots = max(2, (needed + nshard - 1) // nshard)
    double_width = 2 * feature_width
    score_scale = 1.0 / math.sqrt(HEAD_SIZE)
    paired = jnp.concatenate([key_states, values], axis=1)
    paired_blocks = paired.reshape(block_count, BLOCK_TOKENS, double_width)
    extended = extended_2(paired, (("seq", 0),), BLOCK_TOKENS)
    owners_glob = global_blocks // block_count
    local_glob = global_blocks % block_count
    pieces = []
    for glob_index in range(nglob):
        piece = lax.dynamic_slice_in_dim(
            paired, local_glob[glob_index] * BLOCK_TOKENS, BLOCK_TOKENS, 0
        )
        pieces.append(jnp.where(owners_glob[glob_index] == myself, piece.astype(jnp.float32), 0.0))
    global_rows = lax.psum(jnp.concatenate(pieces, axis=0), "seq").astype(jnp.bfloat16)
    table = rand_blocks.reshape(nshard, needed)
    owner_table = table // block_count
    local_table = table % block_count
    position = jnp.arange(needed)
    earlier_same = (owner_table[:, :, None] == owner_table[:, None, :]) & (
        position[None, None, :] < position[None, :, None]
    )
    rank_table = jnp.sum(earlier_same.astype(jnp.int32), axis=2)
    slot_range = jnp.arange(slots)
    matched = (owner_table[:, :, None] == myself) & (
        rank_table[:, :, None] == slot_range[None, None, :]
    )
    valid = jnp.any(matched, axis=1)
    send_local = jnp.sum(jnp.where(matched, local_table[:, :, None], 0), axis=1)
    outgoing = jnp.where(
        valid[:, :, None, None], pick_blocks(paired_blocks, send_local), jnp.zeros((), jnp.bfloat16)
    )
    incoming = lax.all_to_all(outgoing, "seq", split_axis=0, concat_axis=0, tiled=True)
    my_owner = lax.dynamic_index_in_dim(owner_table, myself, 0, keepdims=False)
    my_rank = lax.dynamic_index_in_dim(rank_table, myself, 0, keepdims=False)
    flat_slot = my_owner * slots + my_rank
    fetched = pick_blocks(
        incoming.reshape(nshard * slots, BLOCK_TOKENS, double_width), flat_slot
    ).reshape(block_count, nrand, BLOCK_TOKENS, double_width)
    ext_blocks = extended.reshape(block_count + 2, BLOCK_TOKENS, double_width)
    window_blocks = jnp.stack([ext_blocks[:-2], ext_blocks[1:-1], ext_blocks[2:]], axis=1)
    glob_wide = jnp.broadcast_to(
        global_rows.reshape(1, nglob, BLOCK_TOKENS, double_width),
        (block_count, nglob, BLOCK_TOKENS, double_width),
    )
    gathered = jnp.concatenate([window_blocks, glob_wide, fetched], axis=1)
    key_count = gathered.shape[1]
    key_matrix = gathered[..., :feature_width].reshape(
        block_count, key_count * BLOCK_TOKENS, head_count, HEAD_SIZE
    )
    value_matrix = gathered[..., feature_width:].reshape(
        block_count, key_count * BLOCK_TOKENS, head_count, HEAD_SIZE
    )
    query_matrix = query.reshape(block_count, BLOCK_TOKENS, head_count, HEAD_SIZE)
    logit_scores = (
        jnp.einsum("bqhd,bkhd->bhqk", query_matrix, key_matrix, preferred_element_type=jnp.float32)
        * score_scale
    )
    top = jnp.max(logit_scores, axis=-1, keepdims=True)
    lse = top + jnp.log(jnp.sum(jnp.exp(logit_scores - top), axis=-1, keepdims=True))
    probs = jnp.exp(logit_scores - lse)
    softmax_weights = probs.astype(jnp.bfloat16)
    attended_output = jnp.einsum(
        "bhqk,bkhd->bqhd", softmax_weights, value_matrix, preferred_element_type=jnp.float32
    ).astype(jnp.bfloat16)
    out = attended_output.reshape(tokens, feature_width)
    gradient_rows = grad_out.reshape(block_count, BLOCK_TOKENS, head_count, HEAD_SIZE)
    delta = jnp.sum(gradient_rows.astype(jnp.float32) * attended_output.astype(jnp.float32), axis=3)
    delta = jnp.transpose(delta, (0, 2, 1))[..., None]
    probability_gradient = jnp.einsum(
        "bqhd,bkhd->bhqk", gradient_rows, value_matrix, preferred_element_type=jnp.float32
    )
    dscore = (probs * (probability_gradient - delta) * score_scale).astype(jnp.bfloat16)
    query_gradient = jnp.einsum(
        "bhqk,bkhd->bqhd", dscore, key_matrix, preferred_element_type=jnp.float32
    ).astype(jnp.bfloat16)
    query_gradient = query_gradient.reshape(tokens, feature_width)
    key_term = jnp.einsum(
        "bhqk,bqhd->bkhd", dscore, query_matrix, preferred_element_type=jnp.float32
    )
    value_term = jnp.einsum(
        "bhqk,bqhd->bkhd", softmax_weights, gradient_rows, preferred_element_type=jnp.float32
    )
    terms = jnp.concatenate(
        [
            key_term.reshape(block_count, key_count, BLOCK_TOKENS, feature_width),
            value_term.reshape(block_count, key_count, BLOCK_TOKENS, feature_width),
        ],
        axis=3,
    )
    zero_one = jnp.zeros((1, BLOCK_TOKENS, double_width), jnp.float32)
    zero_two = jnp.zeros((2, BLOCK_TOKENS, double_width), jnp.float32)
    ext_grad = (
        jnp.concatenate([terms[:, 0], zero_two], axis=0)
        + jnp.concatenate([zero_one, terms[:, 1], zero_one], axis=0)
        + jnp.concatenate([zero_two, terms[:, 2]], axis=0)
    )
    rims = jnp.concatenate([ext_grad[0], ext_grad[-1]], axis=0)
    returned = extended_2(rims, (("seq", 0),), BLOCK_TOKENS)
    own = ext_grad[1:-1]
    own = own.at[0].add(returned[:BLOCK_TOKENS]).at[-1].add(returned[3 * BLOCK_TOKENS :])
    glob_terms = jnp.sum(terms[:, 3:nfixed], axis=0)
    glob_total = lax.psum(glob_terms, "seq")
    block_ids = jnp.arange(block_count)
    for glob_index in range(nglob):
        owned_here = (block_ids == local_glob[glob_index]) & (owners_glob[glob_index] == myself)
        own = own + jnp.where(owned_here[:, None, None], glob_total[glob_index][None], 0.0)
    tile_terms = terms[:, nfixed:].reshape(needed, BLOCK_TOKENS, double_width).astype(jnp.bfloat16)
    empty = jnp.zeros((nshard * slots,) + tile_terms.shape[1:], tile_terms.dtype)
    arrived = lax.all_to_all(
        empty.at[flat_slot].set(tile_terms).reshape((nshard, slots) + tile_terms.shape[1:]),
        "seq",
        split_axis=0,
        concat_axis=0,
        tiled=True,
    )
    selector = (send_local.reshape(-1)[None, :] == block_ids[:, None]) & valid.reshape(-1)[None, :]
    own = own + jnp.einsum(
        "bs,sqc->bqc",
        selector.astype(jnp.bfloat16),
        arrived.reshape(nshard * slots, BLOCK_TOKENS, double_width),
        preferred_element_type=jnp.float32,
    )
    own = own.reshape(tokens, double_width)
    dkey = own[:, :feature_width].astype(jnp.bfloat16)
    dvalue = own[:, feature_width:].astype(jnp.bfloat16)
    return (out, query_gradient, dkey, dvalue)


PAIRS = 4
SIDE = 2 * HEAD_SIZE
MASKED = -1e30
NT = (((1,), (1,)), ((), ()))
TN = (((0,), (0,)), ((), ()))
NN = (((1,), (0,)), ((), ()))


def dot(a, b, dims):
    return lax.dot_general(a, b, dims, preferred_element_type=jnp.float32)


def fused_kernel(
    rand_ref, glob_ref, q_ref, k_ref, v_ref, g_ref,
    res_ref,
    kv, own, qg, pack, bias, score, dprob, top, total, acc_out, acc_dq,
    part, cross, cross_in, line, line_in, swap_out, swap_in,
    loaded, line_sent, cross_sent, kv_got, swap_sent, swap_got,
    grad_cross_sent, grad_cross_got, grad_line_sent, grad_line_got,
):
    tokens = q_ref.shape[0]
    rows = 2 * tokens
    blocks = tokens // BLOCK_TOKENS
    nrand = rand_ref.shape[0]
    nglob = glob_ref.shape[0]
    block_total = rand_ref.shape[1]
    scale = 1.0 / math.sqrt(HEAD_SIZE)
    scale2 = scale * math.log2(math.e)

    s = lax.axis_index("seq")
    z, x = s // 2, s % 2
    partner = s + 1 - 2 * x
    zq = z % 2
    mate = z + 1 - 2 * zq
    skip = (z + 2) % PAIRS
    mirror = PAIRS - 1 - z
    head = ((z + 1) // 2) % 2
    tour = (skip, mirror, mate)

    def remote(src, dst, sent, got, to):
        return pltpu.make_async_remote_copy(
            src_ref=src, dst_ref=dst, send_sem=sent, recv_sem=got,
            device_id={"seq": to}, device_id_type=pl.DeviceIdType.MESH,
        )

    def kv_line(zz):
        their_head = ((zz + 1) // 2) % 2
        return remote(own.at[their_head], kv.at[s], line_sent.at[zz], kv_got.at[s], 2 * zz + x)

    def kv_cross(zz):
        slot = 2 * zz + x
        return remote(kv.at[slot], kv.at[slot], cross_sent.at[zz], kv_got.at[slot], partner)

    def kv_arrival(slot):
        return remote(kv.at[slot], kv.at[slot], cross_sent.at[0], kv_got.at[slot], partner)

    to_mate = 2 * mate + x
    qg_swap = remote(pack, qg.at[zq], swap_sent.at[0], swap_got.at[0], to_mate)
    o_swap = remote(swap_out.at[0], swap_in.at[0], swap_sent.at[1], swap_got.at[1], to_mate)
    q_swap = remote(swap_out.at[1], swap_in.at[1], swap_sent.at[2], swap_got.at[2], to_mate)

    def grad_cross(zz):
        return remote(
            cross.at[zz], cross_in.at[zz], grad_cross_sent.at[zz], grad_cross_got.at[zz], partner
        )

    def grad_line(zz):
        return remote(
            line.at[zz], line_in.at[z], grad_line_sent.at[zz], grad_line_got.at[z], 2 * zz + x
        )

    def grad_arrival(zz):
        return remote(
            line.at[zz], line_in.at[zz], grad_line_sent.at[zz], grad_line_got.at[zz], 2 * zz + x
        )

    mine = pl.ds(pl.multiple_of(head * HEAD_SIZE, HEAD_SIZE), HEAD_SIZE)
    theirs = pl.ds(pl.multiple_of((1 - head) * HEAD_SIZE, HEAD_SIZE), HEAD_SIZE)
    low, high = pl.ds(0, HEAD_SIZE), pl.ds(HEAD_SIZE, HEAD_SIZE)
    loads = []
    for src, lanes, dst in (
        (q_ref, theirs, pack.at[:, low]), (g_ref, theirs, pack.at[:, high]),
        (k_ref, low, own.at[0, :, low]), (v_ref, low, own.at[0, :, high]),
        (k_ref, high, own.at[1, :, low]), (v_ref, high, own.at[1, :, high]),
        (k_ref, mine, kv.at[s, :, low]), (v_ref, mine, kv.at[s, :, high]),
        (q_ref, mine, qg.at[zq, :, low]), (g_ref, mine, qg.at[zq, :, high]),
    ):
        loads.append(pltpu.make_async_copy(src.at[:, lanes], dst, loaded.at[len(loads)]))
        loads[-1].start()

    barrier = pltpu.get_barrier_semaphore()
    for to in (partner, to_mate, 2 * skip + x, 2 * mirror + x):
        pl.semaphore_signal(
            barrier, inc=1, device_id={"seq": to}, device_id_type=pl.DeviceIdType.MESH
        )
    pl.semaphore_wait(barrier, 4)
    loads[0].wait()
    loads[1].wait()
    qg_swap.start()
    for load in loads[2:8]:
        load.wait()
    kv_cross(z).start()
    for zz in tour:
        kv_line(zz).start()

    lane_shard = lax.broadcasted_iota(jnp.int32, (1, rows), 1) // tokens
    lane_block = lax.broadcasted_iota(jnp.int32, (1, rows), 1) // BLOCK_TOKENS
    base = 4 * (z // 2) + x
    block = (base + 2 * lane_shard) * blocks + lane_block - lane_shard * blocks
    entries = [
        jnp.where(block == 0, block_total - 1, block - 1),
        block,
        jnp.where(block == block_total - 1, 0, block + 1),
    ]
    for j in range(nglob):
        entries.append(jnp.full((1, rows), glob_ref[j], jnp.int32))
    for j in range(nrand):
        entry = jnp.zeros((1, rows), jnp.int32)
        for i in range(2 * blocks):
            there = (base + 2 * (i // blocks)) * blocks + i % blocks
            entry = jnp.where(lane_block == i, rand_ref[j, there], entry)
        entries.append(entry)
    key_block = lax.broadcasted_iota(jnp.int32, (block_total, rows), 0)
    count = jnp.zeros((block_total, rows), jnp.float32)
    for entry in entries:
        count = count + jnp.where(key_block == entry, 1.0, 0.0)
    bias_all = jnp.where(count > 0.0, jnp.log2(jnp.maximum(count, 1.0)), MASKED)
    for j in range(2 * PAIRS):
        bias[j] = bias_all[j * blocks : (j + 1) * blocks]

    top[...] = jnp.full_like(top, MASKED)
    total[...] = jnp.zeros_like(total)
    acc_out[...] = jnp.zeros_like(acc_out)
    acc_dq[...] = jnp.zeros_like(acc_dq)
    loads[8].wait()
    loads[9].wait()
    remote(pack, qg.at[1 - zq], swap_sent.at[0], swap_got.at[0], to_mate).wait_recv()

    def queries():
        return qg[:, :, :HEAD_SIZE].reshape(rows, HEAD_SIZE)

    def grads():
        return qg[:, :, HEAD_SIZE:].reshape(rows, HEAD_SIZE)

    def tour_at(i):
        return jnp.where(i == 0, skip, jnp.where(i == 1, mirror, jnp.where(i == 2, mate, z)))

    def forward(slot):
        key = kv[slot, :, :HEAD_SIZE]
        value = kv[slot, :, HEAD_SIZE:]
        st = dot(key, queries(), NT) * scale2
        st = (st.reshape(blocks, BLOCK_TOKENS, rows) + bias[slot][:, None, :]).reshape(tokens, rows)
        score[slot] = st
        old = top[...]
        new = jnp.maximum(old, jnp.max(st, axis=0, keepdims=True))
        e = jnp.exp2(st - new)
        alpha = jnp.exp2(old - new)
        top[...] = new
        total[...] = total[...] * alpha + jnp.sum(e, axis=0, keepdims=True)
        acc_out[...] = acc_out[...] * alpha + dot(value, e.astype(jnp.bfloat16), TN)
        dprob[slot] = dot(value, grads(), NT)

    @pl.loop(0, 8)
    def _(i):
        zz = jnp.where(i < 2, z, tour_at((i - 2) % 3))
        column = jnp.where((i == 1) | (i > 4), 1 - x, x)
        slot = 2 * zz + column

        @pl.when(i > 0)
        def _():
            kv_arrival(slot).wait_recv()

        @pl.when((i >= 2) & (i <= 4))
        def _():
            kv_cross(zz).start()

        forward(slot)

    lse = top[...] + jnp.log2(total[...])
    out_t = (acc_out[...] / total[...]).astype(jnp.bfloat16).astype(jnp.float32)
    grad_t = grads().astype(jnp.float32).T
    delta = jnp.sum(out_t * grad_t, axis=0, keepdims=True)
    acc_out[...] = out_t
    top[...] = lse
    total[...] = delta

    def backward(slot):
        prob = jnp.exp2(score[slot] - top[...])
        ds = (prob * (dprob[slot] - total[...]) * scale).astype(jnp.bfloat16)
        dk_term = dot(ds, queries(), NN)
        dv_term = dot(prob.astype(jnp.bfloat16), grads(), NN)
        return ds, dk_term, dv_term

    def add_dq(slot, ds):
        acc_dq[...] += dot(kv[slot, :, :HEAD_SIZE], ds, TN)

    @pl.loop(0, 4)
    def _(i):
        zz = tour_at(i)
        slot = 2 * zz + 1 - x
        ds, dk_term, dv_term = backward(slot)
        cross[zz, :, :HEAD_SIZE] = dk_term.astype(jnp.bfloat16)
        cross[zz, :, HEAD_SIZE:] = dv_term.astype(jnp.bfloat16)
        grad_cross(zz).start()
        add_dq(slot, ds)

    def hand_back(which, rows_t, swap):
        turned = rows_t.T.astype(jnp.bfloat16)
        first, second = turned[:tokens], turned[tokens:]
        swap_out[which] = jnp.where(zq == 0, second, first)
        res_ref[which, :, mine] = jnp.where(zq == 0, first, second)
        swap.start()

    hand_back(0, acc_out[...], o_swap)

    @pl.loop(0, 4)
    def _(i):
        zz = tour_at(i)
        slot = 2 * zz + x
        ds, dk_term, dv_term = backward(slot)
        part[zz, :, :HEAD_SIZE] = dk_term
        part[zz, :, HEAD_SIZE:] = dv_term
        add_dq(slot, ds)

        @pl.when(i < 3)
        def _():
            grad_cross(zz).wait_recv()
            added = part[zz] + cross_in[zz].astype(jnp.float32)
            line[zz] = added.astype(jnp.bfloat16)
            grad_line(zz).start()

    hand_back(1, acc_dq[...], q_swap)

    grad_cross(z).wait_recv()
    grad_arrival(mirror).wait_recv()
    same = part[z] + cross_in[z].astype(jnp.float32) + line_in[mirror].astype(jnp.float32)
    res_ref[2, :, mine] = same[:, :HEAD_SIZE].astype(jnp.bfloat16)
    res_ref[3, :, mine] = same[:, HEAD_SIZE:].astype(jnp.bfloat16)

    qg_swap.wait_send()
    kv_cross(z).wait_send()
    for zz in tour:
        kv_line(zz).wait_send()
        kv_cross(zz).wait_send()
    o_swap.wait()
    res_ref[0, :, theirs] = swap_in[0]
    q_swap.wait()
    res_ref[1, :, theirs] = swap_in[1]
    grad_arrival(skip).wait_recv()
    grad_arrival(mate).wait_recv()
    other = line_in[skip].astype(jnp.float32) + line_in[mate].astype(jnp.float32)
    res_ref[2, :, theirs] = other[:, :HEAD_SIZE].astype(jnp.bfloat16)
    res_ref[3, :, theirs] = other[:, HEAD_SIZE:].astype(jnp.bfloat16)
    for zz in tour:
        grad_cross(zz).wait_send()
        grad_line(zz).wait_send()
    grad_cross(z).wait_send()


def split_kernel(res_ref, o_ref, dq_ref, dk_ref, dv_ref, held, sems):
    loads = [
        pltpu.make_async_copy(res_ref.at[i], held.at[i], sems.at[i]) for i in range(4)
    ]
    stores = [
        pltpu.make_async_copy(held.at[i], dst, sems.at[4 + i])
        for i, dst in enumerate((o_ref, dq_ref, dk_ref, dv_ref))
    ]
    for load in loads:
        load.start()
    for load, store in zip(loads, stores):
        load.wait()
        store.start()
    for store in stores:
        store.wait()


def fused(query, key_states, values, grad_out, rand_blocks, global_blocks):
    tokens = query.shape[0]
    rows = 2 * tokens
    slots = 2 * PAIRS
    blocks = tokens // BLOCK_TOKENS
    bf16, f32 = jnp.bfloat16, jnp.float32
    vmem = pl.BlockSpec(memory_space=pltpu.VMEM)
    smem = pl.BlockSpec(memory_space=pltpu.SMEM)
    hbm = pl.BlockSpec(memory_space=pl.ANY)
    dma = pltpu.SemaphoreType.DMA
    work = 6 * 2 * rows * slots * tokens * HEAD_SIZE
    piece = (tokens, SIDE)
    results = pl.pallas_call(
        fused_kernel,
        out_shape=jax.ShapeDtypeStruct((4,) + query.shape, bf16),
        in_specs=[smem, smem, hbm, hbm, hbm, hbm],
        out_specs=vmem,
        scratch_shapes=[
            pltpu.VMEM((slots,) + piece, bf16),
            pltpu.VMEM((2,) + piece, bf16),
            pltpu.VMEM((2,) + piece, bf16),
            pltpu.VMEM(piece, bf16),
            pltpu.VMEM((slots, blocks, rows), f32),
            pltpu.VMEM((slots, tokens, rows), f32),
            pltpu.VMEM((slots, tokens, rows), f32),
            pltpu.VMEM((1, rows), f32),
            pltpu.VMEM((1, rows), f32),
            pltpu.VMEM((HEAD_SIZE, rows), f32),
            pltpu.VMEM((HEAD_SIZE, rows), f32),
            pltpu.VMEM((PAIRS,) + piece, f32),
            pltpu.VMEM((PAIRS,) + piece, bf16),
            pltpu.VMEM((PAIRS,) + piece, bf16),
            pltpu.VMEM((PAIRS,) + piece, bf16),
            pltpu.VMEM((PAIRS,) + piece, bf16),
            pltpu.VMEM((2, tokens, HEAD_SIZE), bf16),
            pltpu.VMEM((2, tokens, HEAD_SIZE), bf16),
            dma((10,)), dma((PAIRS,)), dma((PAIRS,)), dma((slots,)), dma((3,)), dma((3,)),
            dma((PAIRS,)), dma((PAIRS,)), dma((PAIRS,)), dma((PAIRS,)),
        ],
        compiler_params=pltpu.CompilerParams(
            collective_id=0, has_side_effects=True, vmem_limit_bytes=60 * 1024 * 1024
        ),
        cost_estimate=pl.CostEstimate(
            flops=work, bytes_accessed=8 * tokens * SIDE * 2, transcendentals=2 * rows * slots * tokens
        ),
    )(rand_blocks.T, global_blocks, query, key_states, values, grad_out)
    anywhere = pl.BlockSpec(memory_space=pl.ANY)
    return pl.pallas_call(
        split_kernel,
        out_shape=[jax.ShapeDtypeStruct(query.shape, bf16)] * 4,
        in_specs=[anywhere],
        out_specs=[hbm] * 4,
        scratch_shapes=[pltpu.VMEM((4,) + query.shape, bf16), dma((8,))],
        cost_estimate=pl.CostEstimate(
            flops=0, bytes_accessed=16 * tokens * SIDE, transcendentals=0
        ),
    )(results)


def device_program(query, key_states, values, grad_out, rand_blocks, global_blocks):
    if lax.axis_size("seq") == 2 * PAIRS and query.shape == (4 * BLOCK_TOKENS, 2 * HEAD_SIZE):
        return tuple(fused(query, key_states, values, grad_out, rand_blocks, global_blocks))
    return shards(query, key_states, values, grad_out, rand_blocks, global_blocks)


def solution(mesh):
    in_specs = (P("seq", "head"), P("seq", "head"), P("seq", "head"), P("seq", "head"), P(), P())
    out_specs = (P("seq", "head"), P("seq", "head"), P("seq", "head"), P("seq", "head"))
    return jax.shard_map(
        device_program, mesh=mesh, in_specs=in_specs, out_specs=out_specs, check_vma=False
    )
```

```python
import math

import jax
import jax.numpy as jnp
from jax import lax
from jax.experimental import pallas as pl
from jax.experimental.pallas import tpu as pltpu
from jax.sharding import PartitionSpec as P

HEAD_SIZE = 128
BLOCK_TOKENS = 64


def extended_2(block, sides, width):
    for axis, dim in sides:
        count = lax.axis_size(axis)
        forward = [(i, i + 1) for i in range(count - 1)]
        forward.append((count - 1, 0))
        backward = [(target, source) for source, target in forward]
        low = lax.ppermute(
            lax.slice_in_dim(block, block.shape[dim] - width, None, axis=dim), axis, forward
        )
        high = lax.ppermute(lax.slice_in_dim(block, 0, width, axis=dim), axis, backward)
        block = jnp.concatenate([low, block, high], axis=dim)
    return block


def pick_blocks(blocks, index):
    onehot = (index[..., None] == jnp.arange(blocks.shape[0])).astype(blocks.dtype)
    picked = jnp.einsum(
        "...b,bqc->...qc", onehot, blocks, preferred_element_type=jnp.float32
    )
    return picked.astype(blocks.dtype)


def shards(query, key_states, values, grad_out, rand_blocks, global_blocks):
    tokens, feature_width = query.shape
    head_count = feature_width // HEAD_SIZE
    nshard = lax.axis_size("seq")
    myself = lax.axis_index("seq")
    block_count = tokens // BLOCK_TOKENS
    nrand = rand_blocks.shape[1]
    nglob = global_blocks.shape[0]
    nfixed = 3 + nglob
    needed = block_count * nrand
    slots = max(2, (needed + nshard - 1) // nshard)
    double_width = 2 * feature_width
    score_scale = 1.0 / math.sqrt(HEAD_SIZE)
    paired = jnp.concatenate([key_states, values], axis=1)
    paired_blocks = paired.reshape(block_count, BLOCK_TOKENS, double_width)
    extended = extended_2(paired, (("seq", 0),), BLOCK_TOKENS)
    owners_glob = global_blocks // block_count
    local_glob = global_blocks % block_count
    pieces = []
    for glob_index in range(nglob):
        piece = lax.dynamic_slice_in_dim(
            paired, local_glob[glob_index] * BLOCK_TOKENS, BLOCK_TOKENS, 0
        )
        pieces.append(jnp.where(owners_glob[glob_index] == myself, piece.astype(jnp.float32), 0.0))
    global_rows = lax.psum(jnp.concatenate(pieces, axis=0), "seq").astype(jnp.bfloat16)
    table = rand_blocks.reshape(nshard, needed)
    owner_table = table // block_count
    local_table = table % block_count
    position = jnp.arange(needed)
    earlier_same = (owner_table[:, :, None] == owner_table[:, None, :]) & (
        position[None, None, :] < position[None, :, None]
    )
    rank_table = jnp.sum(earlier_same.astype(jnp.int32), axis=2)
    slot_range = jnp.arange(slots)
    matched = (owner_table[:, :, None] == myself) & (
        rank_table[:, :, None] == slot_range[None, None, :]
    )
    valid = jnp.any(matched, axis=1)
    send_local = jnp.sum(jnp.where(matched, local_table[:, :, None], 0), axis=1)
    outgoing = jnp.where(
        valid[:, :, None, None], pick_blocks(paired_blocks, send_local), jnp.zeros((), jnp.bfloat16)
    )
    incoming = lax.all_to_all(outgoing, "seq", split_axis=0, concat_axis=0, tiled=True)
    my_owner = lax.dynamic_index_in_dim(owner_table, myself, 0, keepdims=False)
    my_rank = lax.dynamic_index_in_dim(rank_table, myself, 0, keepdims=False)
    flat_slot = my_owner * slots + my_rank
    fetched = pick_blocks(
        incoming.reshape(nshard * slots, BLOCK_TOKENS, double_width), flat_slot
    ).reshape(block_count, nrand, BLOCK_TOKENS, double_width)
    ext_blocks = extended.reshape(block_count + 2, BLOCK_TOKENS, double_width)
    window_blocks = jnp.stack([ext_blocks[:-2], ext_blocks[1:-1], ext_blocks[2:]], axis=1)
    glob_wide = jnp.broadcast_to(
        global_rows.reshape(1, nglob, BLOCK_TOKENS, double_width),
        (block_count, nglob, BLOCK_TOKENS, double_width),
    )
    gathered = jnp.concatenate([window_blocks, glob_wide, fetched], axis=1)
    key_count = gathered.shape[1]
    key_matrix = gathered[..., :feature_width].reshape(
        block_count, key_count * BLOCK_TOKENS, head_count, HEAD_SIZE
    )
    value_matrix = gathered[..., feature_width:].reshape(
        block_count, key_count * BLOCK_TOKENS, head_count, HEAD_SIZE
    )
    query_matrix = query.reshape(block_count, BLOCK_TOKENS, head_count, HEAD_SIZE)
    logit_scores = (
        jnp.einsum("bqhd,bkhd->bhqk", query_matrix, key_matrix, preferred_element_type=jnp.float32)
        * score_scale
    )
    top = jnp.max(logit_scores, axis=-1, keepdims=True)
    lse = top + jnp.log(jnp.sum(jnp.exp(logit_scores - top), axis=-1, keepdims=True))
    probs = jnp.exp(logit_scores - lse)
    softmax_weights = probs.astype(jnp.bfloat16)
    attended_output = jnp.einsum(
        "bhqk,bkhd->bqhd", softmax_weights, value_matrix, preferred_element_type=jnp.float32
    ).astype(jnp.bfloat16)
    out = attended_output.reshape(tokens, feature_width)
    gradient_rows = grad_out.reshape(block_count, BLOCK_TOKENS, head_count, HEAD_SIZE)
    delta = jnp.sum(gradient_rows.astype(jnp.float32) * attended_output.astype(jnp.float32), axis=3)
    delta = jnp.transpose(delta, (0, 2, 1))[..., None]
    probability_gradient = jnp.einsum(
        "bqhd,bkhd->bhqk", gradient_rows, value_matrix, preferred_element_type=jnp.float32
    )
    dscore = (probs * (probability_gradient - delta) * score_scale).astype(jnp.bfloat16)
    query_gradient = jnp.einsum(
        "bhqk,bkhd->bqhd", dscore, key_matrix, preferred_element_type=jnp.float32
    ).astype(jnp.bfloat16)
    query_gradient = query_gradient.reshape(tokens, feature_width)
    key_term = jnp.einsum(
        "bhqk,bqhd->bkhd", dscore, query_matrix, preferred_element_type=jnp.float32
    )
    value_term = jnp.einsum(
        "bhqk,bqhd->bkhd", softmax_weights, gradient_rows, preferred_element_type=jnp.float32
    )
    terms = jnp.concatenate(
        [
            key_term.reshape(block_count, key_count, BLOCK_TOKENS, feature_width),
            value_term.reshape(block_count, key_count, BLOCK_TOKENS, feature_width),
        ],
        axis=3,
    )
    zero_one = jnp.zeros((1, BLOCK_TOKENS, double_width), jnp.float32)
    zero_two = jnp.zeros((2, BLOCK_TOKENS, double_width), jnp.float32)
    ext_grad = (
        jnp.concatenate([terms[:, 0], zero_two], axis=0)
        + jnp.concatenate([zero_one, terms[:, 1], zero_one], axis=0)
        + jnp.concatenate([zero_two, terms[:, 2]], axis=0)
    )
    rims = jnp.concatenate([ext_grad[0], ext_grad[-1]], axis=0)
    returned = extended_2(rims, (("seq", 0),), BLOCK_TOKENS)
    own = ext_grad[1:-1]
    own = own.at[0].add(returned[:BLOCK_TOKENS]).at[-1].add(returned[3 * BLOCK_TOKENS :])
    glob_terms = jnp.sum(terms[:, 3:nfixed], axis=0)
    glob_total = lax.psum(glob_terms, "seq")
    block_ids = jnp.arange(block_count)
    for glob_index in range(nglob):
        owned_here = (block_ids == local_glob[glob_index]) & (owners_glob[glob_index] == myself)
        own = own + jnp.where(owned_here[:, None, None], glob_total[glob_index][None], 0.0)
    tile_terms = terms[:, nfixed:].reshape(needed, BLOCK_TOKENS, double_width).astype(jnp.bfloat16)
    empty = jnp.zeros((nshard * slots,) + tile_terms.shape[1:], tile_terms.dtype)
    arrived = lax.all_to_all(
        empty.at[flat_slot].set(tile_terms).reshape((nshard, slots) + tile_terms.shape[1:]),
        "seq",
        split_axis=0,
        concat_axis=0,
        tiled=True,
    )
    selector = (send_local.reshape(-1)[None, :] == block_ids[:, None]) & valid.reshape(-1)[None, :]
    own = own + jnp.einsum(
        "bs,sqc->bqc",
        selector.astype(jnp.bfloat16),
        arrived.reshape(nshard * slots, BLOCK_TOKENS, double_width),
        preferred_element_type=jnp.float32,
    )
    own = own.reshape(tokens, double_width)
    dkey = own[:, :feature_width].astype(jnp.bfloat16)
    dvalue = own[:, feature_width:].astype(jnp.bfloat16)
    return (out, query_gradient, dkey, dvalue)


PAIRS = 4
SIDE = 2 * HEAD_SIZE
MASKED = -1e30
NT = (((1,), (1,)), ((), ()))
TN = (((0,), (0,)), ((), ()))
NN = (((1,), (0,)), ((), ()))


def dot(a, b, dims):
    return lax.dot_general(a, b, dims, preferred_element_type=jnp.float32)


def fused_kernel(
    rand_ref, glob_ref, q_ref, k_ref, v_ref, g_ref,
    res_ref,
    kv, own, qg, pack, bias, score, dprob, top, total, acc_out, acc_dq,
    part, cross, cross_in, line, line_in, swap_out, swap_in,
    loaded, line_sent, cross_sent, kv_got, swap_sent, swap_got,
    grad_cross_sent, grad_cross_got, grad_line_sent, grad_line_got,
):
    tokens = q_ref.shape[0]
    rows = 2 * tokens
    blocks = tokens // BLOCK_TOKENS
    nrand = rand_ref.shape[0]
    nglob = glob_ref.shape[0]
    block_total = rand_ref.shape[1]
    scale = 1.0 / math.sqrt(HEAD_SIZE)
    scale2 = scale * math.log2(math.e)

    s = lax.axis_index("seq")
    z, x = s // 2, s % 2
    partner = s + 1 - 2 * x
    zq = z % 2
    mate = z + 1 - 2 * zq
    skip = (z + 2) % PAIRS
    mirror = PAIRS - 1 - z
    head = ((z + 1) // 2) % 2
    tour = (skip, mirror, mate)
    end = head == 0
    out_order = (jnp.where(end, skip, mirror), jnp.where(end, mirror, mate), jnp.where(end, mate, skip))
    in_order = (jnp.where(end, mate, mirror), jnp.where(end, mirror, skip), jnp.where(end, skip, mate))
    back_order = (jnp.where(end, skip, mate), jnp.where(end, mirror, skip), jnp.where(end, mate, mirror))

    def remote(src, dst, sent, got, to):
        return pltpu.make_async_remote_copy(
            src_ref=src, dst_ref=dst, send_sem=sent, recv_sem=got,
            device_id={"seq": to}, device_id_type=pl.DeviceIdType.MESH,
        )

    def kv_line(zz):
        their_head = ((zz + 1) // 2) % 2
        return remote(own.at[their_head], kv.at[s], line_sent.at[zz], kv_got.at[s], 2 * zz + x)

    def kv_cross(zz):
        slot = 2 * zz + x
        return remote(kv.at[slot], kv.at[slot], cross_sent.at[zz], kv_got.at[slot], partner)

    def kv_arrival(slot):
        return remote(kv.at[slot], kv.at[slot], cross_sent.at[0], kv_got.at[slot], partner)

    to_mate = 2 * mate + x
    qg_swap = remote(pack, qg.at[zq], swap_sent.at[0], swap_got.at[0], to_mate)
    o_swap = remote(swap_out.at[0], swap_in.at[0], swap_sent.at[1], swap_got.at[1], to_mate)
    q_swap = remote(swap_out.at[1], swap_in.at[1], swap_sent.at[2], swap_got.at[2], to_mate)

    def grad_cross(zz):
        return remote(
            cross.at[zz], cross_in.at[zz], grad_cross_sent.at[zz], grad_cross_got.at[zz], partner
        )

    def grad_line(zz):
        return remote(
            line.at[zz], line_in.at[z], grad_line_sent.at[zz], grad_line_got.at[z], 2 * zz + x
        )

    def grad_arrival(zz):
        return remote(
            line.at[zz], line_in.at[zz], grad_line_sent.at[zz], grad_line_got.at[zz], 2 * zz + x
        )

    mine = pl.ds(pl.multiple_of(head * HEAD_SIZE, HEAD_SIZE), HEAD_SIZE)
    theirs = pl.ds(pl.multiple_of((1 - head) * HEAD_SIZE, HEAD_SIZE), HEAD_SIZE)
    low, high = pl.ds(0, HEAD_SIZE), pl.ds(HEAD_SIZE, HEAD_SIZE)
    loads = []
    for src, lanes, dst in (
        (q_ref, theirs, pack.at[:, low]), (g_ref, theirs, pack.at[:, high]),
        (k_ref, low, own.at[0, :, low]), (v_ref, low, own.at[0, :, high]),
        (k_ref, high, own.at[1, :, low]), (v_ref, high, own.at[1, :, high]),
        (k_ref, mine, kv.at[s, :, low]), (v_ref, mine, kv.at[s, :, high]),
        (q_ref, mine, qg.at[zq, :, low]), (g_ref, mine, qg.at[zq, :, high]),
    ):
        loads.append(pltpu.make_async_copy(src.at[:, lanes], dst, loaded.at[len(loads)]))
        loads[-1].start()

    barrier = pltpu.get_barrier_semaphore()
    for to in (partner, to_mate, 2 * skip + x, 2 * mirror + x):
        pl.semaphore_signal(
            barrier, inc=1, device_id={"seq": to}, device_id_type=pl.DeviceIdType.MESH
        )
    pl.semaphore_wait(barrier, 4)
    loads[0].wait()
    loads[1].wait()
    qg_swap.start()
    for load in loads[2:8]:
        load.wait()
    kv_cross(z).start()
    for zz in out_order:
        kv_line(zz).start()

    lane_shard = lax.broadcasted_iota(jnp.int32, (1, rows), 1) // tokens
    lane_block = lax.broadcasted_iota(jnp.int32, (1, rows), 1) // BLOCK_TOKENS
    base = 4 * (z // 2) + x
    block = (base + 2 * lane_shard) * blocks + lane_block - lane_shard * blocks
    entries = [
        jnp.where(block == 0, block_total - 1, block - 1),
        block,
        jnp.where(block == block_total - 1, 0, block + 1),
    ]
    for j in range(nglob):
        entries.append(jnp.full((1, rows), glob_ref[j], jnp.int32))
    for j in range(nrand):
        entry = jnp.zeros((1, rows), jnp.int32)
        for i in range(2 * blocks):
            there = (base + 2 * (i // blocks)) * blocks + i % blocks
            entry = jnp.where(lane_block == i, rand_ref[j, there], entry)
        entries.append(entry)
    key_block = lax.broadcasted_iota(jnp.int32, (block_total, rows), 0)
    count = jnp.zeros((block_total, rows), jnp.float32)
    for entry in entries:
        count = count + jnp.where(key_block == entry, 1.0, 0.0)
    bias_all = jnp.where(count > 0.0, jnp.log2(jnp.maximum(count, 1.0)), MASKED)
    for j in range(2 * PAIRS):
        bias[j] = bias_all[j * blocks : (j + 1) * blocks]

    top[...] = jnp.full_like(top, MASKED)
    total[...] = jnp.zeros_like(total)
    acc_out[...] = jnp.zeros_like(acc_out)
    acc_dq[...] = jnp.zeros_like(acc_dq)
    loads[8].wait()
    loads[9].wait()
    remote(pack, qg.at[1 - zq], swap_sent.at[0], swap_got.at[0], to_mate).wait_recv()

    def queries():
        return qg[:, :, :HEAD_SIZE].reshape(rows, HEAD_SIZE)

    def grads():
        return qg[:, :, HEAD_SIZE:].reshape(rows, HEAD_SIZE)

    def tour_at(i):
        return pick(back_order, i)

    def pick(order, i):
        return jnp.where(i == 0, order[0], jnp.where(i == 1, order[1], jnp.where(i == 2, order[2], z)))

    def forward(slot):
        key = kv[slot, :, :HEAD_SIZE]
        value = kv[slot, :, HEAD_SIZE:]
        st = dot(key, queries(), NT) * scale2
        st = (st.reshape(blocks, BLOCK_TOKENS, rows) + bias[slot][:, None, :]).reshape(tokens, rows)
        score[slot] = st
        old = top[...]
        new = jnp.maximum(old, jnp.max(st, axis=0, keepdims=True))
        e = jnp.exp2(st - new)
        alpha = jnp.exp2(old - new)
        top[...] = new
        total[...] = total[...] * alpha + jnp.sum(e, axis=0, keepdims=True)
        acc_out[...] = acc_out[...] * alpha + dot(value, e.astype(jnp.bfloat16), TN)
        dprob[slot] = dot(value, grads(), NT)

    @pl.loop(0, 8)
    def _(i):
        at = (i - 2) % 3
        zz = jnp.where(i < 2, z, pick(in_order, at))
        column = jnp.where((i == 1) | (i > 4), 1 - x, x)
        slot = 2 * zz + column

        @pl.when(i > 0)
        def _():
            kv_arrival(slot).wait_recv()

        @pl.when((i >= 2) & (i <= 4))
        def _():
            kv_cross(zz).start()

        forward(slot)

    lse = top[...] + jnp.log2(total[...])
    out_t = (acc_out[...] / total[...]).astype(jnp.bfloat16).astype(jnp.float32)
    grad_t = grads().astype(jnp.float32).T
    delta = jnp.sum(out_t * grad_t, axis=0, keepdims=True)
    acc_out[...] = out_t
    top[...] = lse
    total[...] = delta

    def backward(slot):
        prob = jnp.exp2(score[slot] - top[...])
        ds = (prob * (dprob[slot] - total[...]) * scale).astype(jnp.bfloat16)
        dk_term = dot(ds, queries(), NN)
        dv_term = dot(prob.astype(jnp.bfloat16), grads(), NN)
        return ds, dk_term, dv_term

    def add_dq(slot, ds):
        acc_dq[...] += dot(kv[slot, :, :HEAD_SIZE], ds, TN)

    def hand_back(which, rows_t, swap):
        turned = rows_t.T.astype(jnp.bfloat16)
        first, second = turned[:tokens], turned[tokens:]
        swap_out[which] = jnp.where(zq == 0, second, first)
        res_ref[which, :, mine] = jnp.where(zq == 0, first, second)
        swap.start()

    @pl.loop(0, 4)
    def _(i):
        zz = tour_at(i)
        before = tour_at(i - 1)
        slot = 2 * zz + 1 - x
        ds, dk_term, dv_term = backward(slot)
        cross[zz, :, :HEAD_SIZE] = dk_term.astype(jnp.bfloat16)
        cross[zz, :, HEAD_SIZE:] = dv_term.astype(jnp.bfloat16)

        grad_cross(zz).start()
        add_dq(slot, ds)

        @pl.when(i == 0)
        def _():
            hand_back(0, acc_out[...], o_swap)

        slot = 2 * zz + x
        ds, dk_term, dv_term = backward(slot)
        part[zz, :, :HEAD_SIZE] = dk_term
        part[zz, :, HEAD_SIZE:] = dv_term
        add_dq(slot, ds)

        @pl.when(i > 0)
        def _():
            grad_cross(before).wait_recv()
            added = part[before] + cross_in[before].astype(jnp.float32)
            line[before] = added.astype(jnp.bfloat16)

            grad_line(before).start()

    hand_back(1, acc_dq[...], q_swap)

    grad_cross(z).wait_recv()
    grad_arrival(mirror).wait_recv()
    same = part[z] + cross_in[z].astype(jnp.float32) + line_in[mirror].astype(jnp.float32)
    res_ref[2, :, mine] = same[:, :HEAD_SIZE].astype(jnp.bfloat16)
    res_ref[3, :, mine] = same[:, HEAD_SIZE:].astype(jnp.bfloat16)

    kv_cross(z).wait_send()
    qg_swap.wait_send()
    for zz in tour:
        kv_line(zz).wait_send()
    for zz in tour:
        kv_cross(zz).wait_send()
    o_swap.wait()
    res_ref[0, :, theirs] = swap_in[0]
    q_swap.wait()
    res_ref[1, :, theirs] = swap_in[1]
    grad_arrival(skip).wait_recv()
    grad_arrival(mate).wait_recv()
    other = line_in[skip].astype(jnp.float32) + line_in[mate].astype(jnp.float32)
    res_ref[2, :, theirs] = other[:, :HEAD_SIZE].astype(jnp.bfloat16)
    res_ref[3, :, theirs] = other[:, HEAD_SIZE:].astype(jnp.bfloat16)
    for zz in tour:
        grad_cross(zz).wait_send()
        grad_line(zz).wait_send()
    grad_cross(z).wait_send()


def split_kernel(res_ref, o_ref, dq_ref, dk_ref, dv_ref, held, sems):
    loads = [
        pltpu.make_async_copy(res_ref.at[i], held.at[i], sems.at[i]) for i in range(4)
    ]
    stores = [
        pltpu.make_async_copy(held.at[i], dst, sems.at[4 + i])
        for i, dst in enumerate((o_ref, dq_ref, dk_ref, dv_ref))
    ]
    for load in loads:
        load.start()
    for load, store in zip(loads, stores):
        load.wait()
        store.start()
    for store in stores:
        store.wait()


def fused(query, key_states, values, grad_out, rand_blocks, global_blocks):
    tokens = query.shape[0]
    rows = 2 * tokens
    slots = 2 * PAIRS
    blocks = tokens // BLOCK_TOKENS
    bf16, f32 = jnp.bfloat16, jnp.float32
    vmem = pl.BlockSpec(memory_space=pltpu.VMEM)
    smem = pl.BlockSpec(memory_space=pltpu.SMEM)
    hbm = pl.BlockSpec(memory_space=pl.ANY)
    dma = pltpu.SemaphoreType.DMA
    work = 6 * 2 * rows * slots * tokens * HEAD_SIZE
    piece = (tokens, SIDE)
    results = pl.pallas_call(
        fused_kernel,
        out_shape=jax.ShapeDtypeStruct((4,) + query.shape, bf16),
        in_specs=[smem, smem, hbm, hbm, hbm, hbm],
        out_specs=vmem,
        scratch_shapes=[
            pltpu.VMEM((slots,) + piece, bf16),
            pltpu.VMEM((2,) + piece, bf16),
            pltpu.VMEM((2,) + piece, bf16),
            pltpu.VMEM(piece, bf16),
            pltpu.VMEM((slots, blocks, rows), f32),
            pltpu.VMEM((slots, tokens, rows), f32),
            pltpu.VMEM((slots, tokens, rows), f32),
            pltpu.VMEM((1, rows), f32),
            pltpu.VMEM((1, rows), f32),
            pltpu.VMEM((HEAD_SIZE, rows), f32),
            pltpu.VMEM((HEAD_SIZE, rows), f32),
            pltpu.VMEM((PAIRS,) + piece, f32),
            pltpu.VMEM((PAIRS,) + piece, bf16),
            pltpu.VMEM((PAIRS,) + piece, bf16),
            pltpu.VMEM((PAIRS,) + piece, bf16),
            pltpu.VMEM((PAIRS,) + piece, bf16),
            pltpu.VMEM((2, tokens, HEAD_SIZE), bf16),
            pltpu.VMEM((2, tokens, HEAD_SIZE), bf16),
            dma((10,)), dma((PAIRS,)), dma((PAIRS,)), dma((slots,)), dma((3,)), dma((3,)),
            dma((PAIRS,)), dma((PAIRS,)), dma((PAIRS,)), dma((PAIRS,)),
        ],
        compiler_params=pltpu.CompilerParams(
            collective_id=0, has_side_effects=True, vmem_limit_bytes=60 * 1024 * 1024
        ),
        cost_estimate=pl.CostEstimate(
            flops=work, bytes_accessed=8 * tokens * SIDE * 2, transcendentals=2 * rows * slots * tokens
        ),
    )(rand_blocks.T, global_blocks, query, key_states, values, grad_out)
    anywhere = pl.BlockSpec(memory_space=pl.ANY)
    return pl.pallas_call(
        split_kernel,
        out_shape=[jax.ShapeDtypeStruct(query.shape, bf16)] * 4,
        in_specs=[anywhere],
        out_specs=[hbm] * 4,
        scratch_shapes=[pltpu.VMEM((4,) + query.shape, bf16), dma((8,))],
        cost_estimate=pl.CostEstimate(
            flops=0, bytes_accessed=16 * tokens * SIDE, transcendentals=0
        ),
    )(results)


def device_program(query, key_states, values, grad_out, rand_blocks, global_blocks):
    if lax.axis_size("seq") == 2 * PAIRS and query.shape == (4 * BLOCK_TOKENS, 2 * HEAD_SIZE):
        return tuple(fused(query, key_states, values, grad_out, rand_blocks, global_blocks))
    return shards(query, key_states, values, grad_out, rand_blocks, global_blocks)


def solution(mesh):
    in_specs = (P("seq", "head"), P("seq", "head"), P("seq", "head"), P("seq", "head"), P(), P())
    out_specs = (P("seq", "head"), P("seq", "head"), P("seq", "head"), P("seq", "head"))
    return jax.shard_map(
        device_program, mesh=mesh, in_specs=in_specs, out_specs=out_specs, check_vma=False
    )
```
